256 devices in a mesh: dp: 64 (over z, x, core), seq: 4 (over y).
Axes of the slice: x: 4, y: 4, z: 8, core: 2. Of those that a mesh axis runs over, the one named last changes fastest.
Arguments:
- x_saved: bfloat16 [32768, 5120], P(('dp', 'seq')), may hold values from -24 to 24
- q_saved: bfloat16 [32768, 2560], P(('dp', 'seq')), may hold values from -8 to 8
- k_saved: bfloat16 [32768, 512], P(('dp', 'seq')), may hold values from -8 to 8
- grad_attn: bfloat16 [32768, 2560], P(('dp', 'seq')), may hold values from -6 to 6
- token_coef: float32 [32768], P(('dp', 'seq')), may hold values from -4 to 4
- dest_of: int32 [32768], P(('dp', 'seq')), may hold values from 0 to 32767, as said below
- source_of: int32 [32768], P(('dp', 'seq')), may hold values from 0 to 32767, as said below
- lengths: int32 [64, 3], P('dp'), may hold values from 64 to 256, as said below
- value_weight: bfloat16 [5120, 512], P('dp'), may hold values from -0.078125 to 0.078125
Outputs:
- grad_x: bfloat16 [32768, 5120], P(('dp', 'seq'))
- grad_q: bfloat16 [32768, 2560], P(('dp', 'seq'))
- grad_k: bfloat16 [32768, 512], P(('dp', 'seq'))
- grad_v_weight: float32 [5120, 512], P('dp')
The draws below stay inside these ranges and needn't reach their ends.
Inputs may be any that keep to these rules, and one draw needn't show every extreme that they name: dest_of is a permutation that keeps each row at the same index along seq; of the rows of one device, at most 4 go to any one device along dp, and every device sends exactly 4 rows to some device and receives exactly 4 rows from some device. source_of is the inverse permutation of dest_of. The lengths of a group sum to 512; exactly one of them is 256, each other one is at least one eighth of 512.
All inputs are finite; a program needn't handle non-finite values.
Results may differ from the reference program's by a relative error of at most 0.017.
Values may be sent and summed in bfloat16 or wider, within the bound.
No kernel may reach another device: no remote copies, remote signals or barrier semaphores. Data moves between devices by JAX's collectives and lax.ppermute only.
A program may use at most 128 MiB of HBM per device.

```python
import math
import jax
import jax.numpy as jnp
from jax import lax

MODEL_WIDTH = 5120
QUERY_HEADS = 20
KEY_VALUE_HEADS = 4
HEAD_SIZE = 128
ROLLS = 3
TOK_DEV = 128
CAP = 4
GROUP_TOK = 512
TOKEN_COUNT = 32768
MOST = 256
N_DP = 64
N_SEQ = 4


def label_rank(labels, device_ids):
    member = (labels[:, :, None] == device_ids[None, None, :]).astype(jnp.int32)
    return jnp.sum((jnp.cumsum(member, axis=1) - 1) * member, axis=2).astype(jnp.int32)


def column_plan(subkey, column):
    half_cap = CAP // 2
    keys_four = jax.random.split(subkey, 4)
    swings = jax.random.randint(keys_four[0], (N_DP // 2,), -half_cap, half_cap + 1)
    swings = swings.at[0].set(half_cap)
    base_load = jnp.stack([half_cap + swings, half_cap - swings], axis=1).reshape(N_DP)
    base_load = jax.random.permutation(keys_four[1], base_load)
    device_ids = jnp.arange(N_DP, dtype=jnp.int32)
    counts = base_load[(device_ids[None, :] - device_ids[:, None]) % N_DP]

    def listing(count_row, row_key):
        listed = jnp.repeat(device_ids, count_row, total_repeat_length=TOK_DEV)
        return jax.random.permutation(row_key, listed)
    send_label = jax.vmap(listing)(counts, jax.random.split(keys_four[2], N_DP))
    recv_label = jax.vmap(listing)(counts.T, jax.random.split(keys_four[3], N_DP))
    send_rank = label_rank(send_label, device_ids)
    recv_rank = label_rank(recv_label, device_ids)
    owners = jnp.broadcast_to(device_ids[:, None], (N_DP, TOK_DEV))
    positions = jnp.broadcast_to(jnp.arange(TOK_DEV, dtype=jnp.int32)[None, :], (N_DP, TOK_DEV))
    target_spot = jnp.zeros((N_DP, N_DP, CAP), jnp.int32).at[owners, recv_label, recv_rank].set(positions)
    source_spot = jnp.zeros((N_DP, N_DP, CAP), jnp.int32).at[owners, send_label, send_rank].set(positions)
    dest_local = target_spot[send_label, owners, send_rank]
    src_local = source_spot[recv_label, owners, recv_rank]
    dest_global = (send_label * N_SEQ + column) * TOK_DEV + dest_local
    source_global = (recv_label * N_SEQ + column) * TOK_DEV + src_local
    return (dest_global, source_global)


def plan_tables(key):
    plan_key = jax.random.fold_in(key, 101)
    columns = jnp.arange(N_SEQ, dtype=jnp.int32)
    dest_cols, source_cols = jax.vmap(column_plan)(jax.random.split(plan_key, N_SEQ), columns)
    dest_table = jnp.transpose(dest_cols, (1, 0, 2)).reshape(TOKEN_COUNT).astype(jnp.int32)
    source_table = jnp.transpose(source_cols, (1, 0, 2)).reshape(TOKEN_COUNT).astype(jnp.int32)
    length_key = jax.random.fold_in(key, 202)
    middle = jax.random.randint(jax.random.fold_in(length_key, 1), (N_DP,), GROUP_TOK // 8, 3 * GROUP_TOK // 8 + 1)
    pieces = jnp.stack([jnp.full((N_DP,), MOST, jnp.int32), middle.astype(jnp.int32), (GROUP_TOK - MOST - middle).astype(jnp.int32)], axis=1)
    shuffles = jax.vmap(lambda row_key: jax.random.permutation(row_key, ROLLS))(jax.random.split(jax.random.fold_in(length_key, 2), N_DP))
    length_table = jnp.take_along_axis(pieces, shuffles, axis=1).astype(jnp.int32)
    sign_lookup_table = (jax.random.randint(jax.random.fold_in(key, 303), (KEY_VALUE_HEADS, HEAD_SIZE), 0, 2) * 2 - 1).astype(jnp.float32)
    return (dest_table, source_table, length_table, sign_lookup_table)


def draw_dest_of(key, part):
    shared = plan_tables(key)
    return shared[0]


def draw_source_of(key, part):
    shared = plan_tables(key)
    return shared[1]


def draw_lengths(key, part):
    shared = plan_tables(key)
    return shared[2]


def draw_q_saved(key, part):
    key = jax.random.fold_in(key, 11)
    return jnp.clip(jax.random.normal(key, (TOKEN_COUNT, QUERY_HEADS * HEAD_SIZE), jnp.float32), -8.0, 8.0).astype(jnp.bfloat16)


def draw_k_saved(key, part):
    key = jax.random.fold_in(key, 13)
    return jnp.clip(jax.random.normal(key, (TOKEN_COUNT, KEY_VALUE_HEADS * HEAD_SIZE), jnp.float32), -8.0, 8.0).astype(jnp.bfloat16)


def with_spikes(drawn, stream_key, source, target, parts, factor):
    def block_of(dim):
        return (jnp.arange(drawn.shape[dim]) // (drawn.shape[dim] // parts)).reshape((-1,) + (1,) * (drawn.ndim - 1 - dim))

    first = jax.random.permutation(stream_key, parts)[block_of(target)]
    far = (block_of(target) + parts // 2) % parts
    return jnp.where((block_of(source) == first) | (block_of(source) == far), factor * drawn, drawn)


def shard_levels(own_key, dims, cuts, low, largest):
    gain, own = 1.0, jax.random.fold_in(own_key, 6)
    for dim, parts in cuts:
        draws = jnp.exp(jax.random.uniform(jax.random.fold_in(own, dim), (parts,), jnp.float32, low / len(cuts), largest / len(cuts)))
        gain = gain * jnp.repeat(draws, dims[dim] // parts).reshape([-1 if axis == dim else 1 for axis in range(len(dims))])
    return gain


def scatter_about(own_key, dims, scale, reach, cuts=(), held_as=jnp.bfloat16):
    values = scale * jax.random.normal(own_key, dims, jnp.float32)
    if cuts:
        values = values * shard_levels(own_key, dims, cuts, -0.22, 0.18)
    return jnp.clip(values, -reach, reach).astype(held_as)


def gaussian_with(rng, shape, spread, bound, shards, heavy, kind=jnp.bfloat16):
    result = spread * jax.random.normal(rng, shape, jnp.float32)
    if shards:
        result = result * shard_levels(rng, shape, shards, -0.22, 0.18)
    return jnp.clip(with_spikes(result, jax.random.fold_in(rng, 3), *heavy), -bound, bound).astype(kind)


def setup_inputs(seed: int = 0) -> dict:
    arg_keys = jax.random.split(jax.random.key(seed), 10)
    x_saved = gaussian_with(arg_keys[0], (TOKEN_COUNT, MODEL_WIDTH), 1.0, 24.0, ((0, 256),), (0, 1, 256, 6.0))
    q_saved = draw_q_saved(jax.random.fold_in(arg_keys[9], 71), 0)
    k_saved = draw_k_saved(jax.random.fold_in(arg_keys[9], 71), 0)
    grad_attn = scatter_about(arg_keys[3], (TOKEN_COUNT, QUERY_HEADS * HEAD_SIZE), 1.0, 6.0, ((0, 256),))
    token_coef = scatter_about(arg_keys[4], (TOKEN_COUNT,), 1.0, 4.0, ((0, 256),), jnp.float32)
    dest_of = draw_dest_of(jax.random.fold_in(arg_keys[9], 71), 0)
    source_of = draw_source_of(jax.random.fold_in(arg_keys[9], 71), 0)
    lengths = draw_lengths(jax.random.fold_in(arg_keys[9], 71), 0)
    value_weight = scatter_about(arg_keys[8], (MODEL_WIDTH, KEY_VALUE_HEADS * HEAD_SIZE), MODEL_WIDTH ** -0.5, 0.078125, ((0, 64),))
    return dict(x_saved=x_saved, q_saved=q_saved, k_saved=k_saved, grad_attn=grad_attn, token_coef=token_coef, dest_of=dest_of, source_of=source_of, lengths=lengths, value_weight=value_weight)


def rollout_of(position, rollout_ends):
    return lax.optimization_barrier(jnp.sum((position[:, None] >= rollout_ends[None, :]).astype(jnp.int32), axis=1))

def attend_back(q_rows, q_pos, k_rows, v_rows, k_pos, rollout_ends, d_rows):
    rows_q = q_rows.shape[0]
    rows_k = k_rows.shape[0]
    kv_heads = k_rows.shape[1] // HEAD_SIZE
    per_kv = q_rows.shape[1] // (HEAD_SIZE * kv_heads)
    score_scale = HEAD_SIZE ** (-0.5)
    block_rows = 512 if rows_q % 512 == 0 else rows_q
    q_view = q_rows.astype(jnp.float32).reshape(rows_q, kv_heads, per_kv, HEAD_SIZE)
    d_view = d_rows.astype(jnp.float32).reshape(rows_q, kv_heads, per_kv, HEAD_SIZE)
    k_view = k_rows.astype(jnp.float32).reshape(rows_k, kv_heads, HEAD_SIZE)
    v_view = v_rows.astype(jnp.float32).reshape(rows_k, kv_heads, HEAD_SIZE)
    visible_all = (k_pos[None, :] <= q_pos[:, None]) & (rollout_of(k_pos, rollout_ends)[None, :] == rollout_of(q_pos, rollout_ends)[:, None])
    dq_heads = []
    dk_heads = []
    dv_heads = []
    for kv_head in range(kv_heads):
        k_one = k_view[:, kv_head]
        v_one = v_view[:, kv_head]
        dk_total = jnp.zeros((rows_k, HEAD_SIZE), jnp.float32)
        dv_total = jnp.zeros((rows_k, HEAD_SIZE), jnp.float32)
        dq_pieces = []
        for start_row in range(0, rows_q, block_rows):
            q_blk = q_view[start_row:start_row + block_rows, kv_head]
            d_blk = d_view[start_row:start_row + block_rows, kv_head]
            visible = visible_all[start_row:start_row + block_rows]
            scores = jnp.einsum('qgd,kd->gqk', q_blk, k_one) * score_scale
            scores = jnp.where(visible[None], scores, -jnp.inf)
            row_max = lax.optimization_barrier(jnp.max(scores, axis=2, keepdims=True))
            weights = jnp.exp(scores - row_max)
            attn_probs = weights / lax.optimization_barrier(jnp.sum(weights, axis=2, keepdims=True))
            probs_half = lax.optimization_barrier(attn_probs.astype(jnp.bfloat16)).astype(jnp.float32)
            output = jnp.einsum('gqk,kd->qgd', probs_half, v_one)
            row_delta = lax.optimization_barrier(jnp.sum(d_blk * output, axis=2))
            dprobs = jnp.einsum('qgd,kd->gqk', d_blk, v_one)
            dscores = attn_probs * (dprobs - jnp.transpose(row_delta)[:, :, None])
            dscores = lax.optimization_barrier(dscores.astype(jnp.bfloat16)).astype(jnp.float32)
            dq_pieces.append(jnp.einsum('gqk,kd->qgd', dscores, k_one) * score_scale)
            dk_total = dk_total + jnp.einsum('gqk,qgd->kd', dscores, q_blk) * score_scale
            dv_total = dv_total + jnp.einsum('gqk,qgd->kd', probs_half, d_blk)
        dq_heads.append(jnp.concatenate(dq_pieces, axis=0))
        dk_heads.append(dk_total)
        dv_heads.append(dv_total)
    grad_query = jnp.stack(dq_heads, axis=1).reshape(rows_q, -1)
    grad_key = jnp.stack(dk_heads, axis=1).reshape(rows_k, -1)
    grad_value = jnp.stack(dv_heads, axis=1).reshape(rows_k, -1)
    return (grad_query, grad_key, grad_value)

def reference(x_saved, q_saved, k_saved, grad_attn, token_coef, dest_of, source_of, lengths, value_weight):
    values = jnp.dot(x_saved, value_weight, preferred_element_type=jnp.float32)
    values = lax.optimization_barrier(values.astype(jnp.bfloat16))
    weighted = lax.optimization_barrier((token_coef[:, None] * grad_attn.astype(jnp.float32)).astype(jnp.bfloat16))
    q_bal = q_saved[source_of].reshape(N_DP, GROUP_TOK, -1)
    k_bal = k_saved[source_of].reshape(N_DP, GROUP_TOK, -1)
    v_bal = values[source_of].reshape(N_DP, GROUP_TOK, -1)
    d_bal = weighted[source_of].reshape(N_DP, GROUP_TOK, -1)
    group_pos = jnp.arange(GROUP_TOK, dtype=jnp.int32)

    def one_group(inputs):
        q_grp, k_grp, v_grp, d_grp, len_grp = inputs
        rollout_ends = jnp.cumsum(len_grp)
        grad_query, grad_key, grad_value = attend_back(q_grp, group_pos, k_grp, v_grp, group_pos, rollout_ends, d_grp)
        return (grad_query.astype(jnp.bfloat16), grad_key.astype(jnp.bfloat16), grad_value.astype(jnp.bfloat16))
    dq_bal, dk_bal, dv_bal = lax.map(one_group, (q_bal, k_bal, v_bal, d_bal, lengths))
    dq_bal = lax.optimization_barrier(dq_bal)
    grad_q = dq_bal.reshape(TOKEN_COUNT, -1)[dest_of]
    grad_k = dk_bal.reshape(TOKEN_COUNT, -1)[dest_of]
    dv_src = dv_bal.reshape(TOKEN_COUNT, -1)[dest_of]
    grad_x = jnp.dot(dv_src, value_weight.T, preferred_element_type=jnp.float32).astype(jnp.bfloat16)
    grad_v_weight = jnp.dot(x_saved.T, dv_src, preferred_element_type=jnp.float32) / math.sqrt(TOKEN_COUNT)
    return (grad_x, grad_q, grad_k, grad_v_weight)
```

```python
import functools
import math

import jax
import jax.numpy as jnp
from jax import lax
from jax.experimental import pallas as pl
from jax.experimental.pallas import tpu as pltpu
from jax.sharding import PartitionSpec as P

HEAD = 128
CAP = 4
NZ, NX, NC, NS = 8, 4, 2, 4
NDP = NZ * NX * NC
ROWS = 128
GROUP = ROWS * NS
PER = 5
QW = PER * HEAD
BF = jnp.bfloat16
F32 = jnp.float32
SCALE = HEAD ** (-0.5)
LIMIT = 48 * 1024 * 1024

VMEM = pl.BlockSpec(memory_space=pltpu.VMEM)
SMEM = pl.BlockSpec(memory_space=pltpu.SMEM)


def params():
    return pltpu.CompilerParams(vmem_limit_bytes=LIMIT)


def cost(flops, bytes_accessed):
    return pl.CostEstimate(flops=int(flops), bytes_accessed=int(bytes_accessed), transcendentals=0)


def ones_where(hit):
    return jnp.where(hit, 1.0, 0.0).astype(BF)


def mm(a, b):
    return jnp.dot(a, b, preferred_element_type=F32)


def mm_nt(a, b):
    return lax.dot_general(a, b, (((1,), (1,)), ((), ())), preferred_element_type=F32)


def mm_tn(a, b):
    return lax.dot_general(a, b, (((0,), (0,)), ((), ())), preferred_element_type=F32)


def pack_onehot(slots, step):
    row = lax.broadcasted_iota(jnp.int32, (256, ROWS), 0)
    hit = (step * 16 + row // 16) * CAP + row % 4 == slots
    place = (row % 16) // 4
    return jnp.concatenate([ones_where(hit & (place == m)) for m in range(4)], axis=1)


def pack_first_kernel(slots_ref, coef_ref, q_ref, k_ref, g_ref, out_ref):
    onehot = pack_onehot(slots_ref[...], pl.program_id(0))

    def chunk(s, m):
        if m < PER:
            return q_ref[:, s * QW + m * HEAD : s * QW + (m + 1) * HEAD]
        if m == PER:
            return k_ref[:, s * HEAD : (s + 1) * HEAD]
        at = s * QW + (m - PER - 1) * HEAD
        return (coef_ref[...] * g_ref[:, at : at + HEAD].astype(F32)).astype(BF)

    for t in range(2):
        rhs = jnp.concatenate(
            [
                jnp.concatenate([chunk(s, 4 * t + m) for m in range(4)], axis=0)
                for s in range(NS)
            ],
            axis=1,
        )
        res = mm(onehot, rhs).astype(BF)
        for s in range(NS):
            out_ref[:, s, 16 * t : 16 * t + 16, :] = res[:, s * HEAD : (s + 1) * HEAD].reshape(
                16, 16, HEAD
            )


def pack_first(slots, coef, q, k, g):
    return pl.pallas_call(
        pack_first_kernel,
        grid=(4,),
        out_shape=jax.ShapeDtypeStruct((NDP, NS, 32, HEAD), BF),
        in_specs=[
            pl.BlockSpec((1, ROWS), lambda i: (0, 0)),
            pl.BlockSpec((ROWS, 1), lambda i: (0, 0)),
            pl.BlockSpec((ROWS, NS * QW), lambda i: (0, 0)),
            pl.BlockSpec((ROWS, NS * HEAD), lambda i: (0, 0)),
            pl.BlockSpec((ROWS, NS * QW), lambda i: (0, 0)),
        ],
        out_specs=pl.BlockSpec((16, NS, 32, HEAD), lambda i: (i, 0, 0, 0)),
        compiler_params=params(),
        cost_estimate=cost(1.1e9, 4e6),
        name="pack_first",
    )(slots, coef, q, k, g)


def pack_second_kernel(slots_ref, coef_ref, g_ref, v_ref, out_ref):
    onehot = pack_onehot(slots_ref[...], pl.program_id(0))

    def chunk(s, m):
        if m == 3:
            return v_ref[:, s * HEAD : (s + 1) * HEAD]
        at = s * QW + (m + 2) * HEAD
        return (coef_ref[...] * g_ref[:, at : at + HEAD].astype(F32)).astype(BF)

    rhs = jnp.concatenate(
        [jnp.concatenate([chunk(s, m) for m in range(4)], axis=0) for s in range(NS)], axis=1
    )
    res = mm(onehot, rhs).astype(BF)
    for s in range(NS):
        out_ref[:, s, :, :] = res[:, s * HEAD : (s + 1) * HEAD].reshape(16, 16, HEAD)


def pack_second(slots, coef, g, v):
    return pl.pallas_call(
        pack_second_kernel,
        grid=(4,),
        out_shape=jax.ShapeDtypeStruct((NDP, NS, 16, HEAD), BF),
        in_specs=[
            pl.BlockSpec((1, ROWS), lambda i: (0, 0)),
            pl.BlockSpec((ROWS, 1), lambda i: (0, 0)),
            pl.BlockSpec((ROWS, NS * QW), lambda i: (0, 0)),
            pl.BlockSpec((ROWS, NS * HEAD), lambda i: (0, 0)),
        ],
        out_specs=pl.BlockSpec((16, NS, 16, HEAD), lambda i: (i, 0, 0, 0)),
        compiler_params=params(),
        cost_estimate=cost(0.6e9, 2e6),
        name="pack_second",
    )(slots, coef, g, v)


def values_kernel(place_ref, x_ref, *refs):
    pieces, v_ref, w_ref = refs[: NX * NC], refs[NX * NC], refs[NX * NC + 1]
    z, x, c = place_ref[0], place_ref[1], place_ref[2]
    block = w_ref.shape[0] // NDP
    for dx in range(NX):
        for dc in range(NC):
            piece = pieces[dx * NC + dc]
            at_x = lax.rem(x - dx + NX, NX)
            at_c = lax.rem(c + dc, NC)
            for dz in range(NZ):
                at_z = lax.rem(z - dz + NZ, NZ)
                start = pl.multiple_of(((at_z * NX + at_x) * NC + at_c) * block, 16)
                w_ref[pl.ds(start, block), :] = piece[dz]
    v_ref[...] = mm(x_ref[...], w_ref[...]).astype(BF)


def values_of(place, x_saved, pieces):
    depth, width = x_saved.shape[1], pieces[0].shape[2]
    return pl.pallas_call(
        values_kernel,
        out_shape=(
            jax.ShapeDtypeStruct((x_saved.shape[0], width), BF),
            jax.ShapeDtypeStruct((depth, width), BF),
        ),
        in_specs=[SMEM, VMEM] + [VMEM] * len(pieces),
        out_specs=(VMEM, VMEM),
        compiler_params=params(),
        cost_estimate=cost(0.7e9, 12e6),
        name="values",
    )(place, x_saved, *pieces)


def attend_kernel(
    len_ref, slot_col_ref, slot_row_ref, r1_ref, r2_ref, dv_out, dqk_out, qs, ds, ks, vs, dq, dk, dv
):
    for s in range(NS):
        lane = lax.broadcasted_iota(jnp.int32, (ROWS, NDP * 16), 1)
        hit = (lane // 16) * CAP + lane % 4 == slot_col_ref[s * ROWS : (s + 1) * ROWS, :]
        place = (lane % 16) // 4
        pick = jnp.concatenate([ones_where(hit & (place == m)) for m in range(4)], axis=0)
        rhs = jnp.concatenate(
            [
                r1_ref[:, s, 0:16, :].reshape(NDP * 16, HEAD),
                r1_ref[:, s, 16:32, :].reshape(NDP * 16, HEAD),
                r2_ref[:, s, :, :].reshape(NDP * 16, HEAD),
            ],
            axis=1,
        )
        res = mm(pick, rhs).astype(BF)
        qs[s, 0:512, :] = res[:, 0:128]
        qs[s, 512:640, :] = res[0:128, 128:256]
        ks[s * ROWS : (s + 1) * ROWS, :] = res[128:256, 128:256]
        ds[s, 0:256, :] = res[256:512, 128:256]
        ds[s, 256:640, :] = res[0:384, 256:384]
        vs[s * ROWS : (s + 1) * ROWS, :] = res[384:512, 256:384]

    first, second = len_ref[0], len_ref[0] + len_ref[1]
    dk[...] = jnp.zeros_like(dk)
    dv[...] = jnp.zeros_like(dv)
    for s in range(NS):
        lo, hi = max(0, s - 2) * ROWS, (s + 1) * ROWS
        width = hi - lo
        q_pos = s * ROWS + lax.broadcasted_iota(jnp.int32, (ROWS, width), 0)
        k_pos = lo + lax.broadcasted_iota(jnp.int32, (ROWS, width), 1)
        begin = jnp.where(q_pos >= second, second, jnp.where(q_pos >= first, first, 0))
        visible = (k_pos <= q_pos) & (k_pos >= begin)
        q_one, d_one = qs[s], ds[s]
        k_win, v_win = ks[lo:hi, :], vs[lo:hi, :]
        scores = mm_nt(q_one, k_win).reshape(PER, ROWS, width) * SCALE
        scores = jnp.where(visible[None], scores, -jnp.inf)
        weights = jnp.exp(scores - jnp.max(scores, axis=2, keepdims=True))
        probs = weights / jnp.sum(weights, axis=2, keepdims=True)
        half = probs.astype(BF)
        half_two = half.reshape(PER * ROWS, width)
        dv[lo:hi, :] += mm_tn(half_two, d_one)
        dprobs = mm_nt(d_one, v_win).reshape(PER, ROWS, width)
        delta = jnp.sum(half.astype(F32) * dprobs, axis=2, keepdims=True)
        dscores = (probs * (dprobs - delta)).astype(BF).reshape(PER * ROWS, width)
        dq[s] = (mm(dscores, k_win) * SCALE).astype(BF)
        dk[lo:hi, :] += mm_tn(dscores, q_one)

    row = lax.broadcasted_iota(jnp.int32, (NDP * 16, ROWS), 0)
    wanted = (row // 16) * CAP + row % 4
    of_seq = (row % 16) // 4
    spread = jnp.concatenate(
        [ones_where((wanted == slot_row_ref[s : s + 1, :]) & (of_seq == s)) for s in range(NS)],
        axis=1,
    )
    dv_out[...] = mm(spread, dv[...].astype(BF)).astype(BF).reshape(NDP, 16, HEAD)

    row = lax.broadcasted_iota(jnp.int32, (NDP * 8, ROWS), 0)
    wanted = (row // 8) * CAP + row % 4
    place = (row % 8) // 4
    for s in range(NS):
        hit = wanted == slot_row_ref[s : s + 1, :]
        spread = jnp.concatenate([ones_where(hit & (place == m)) for m in range(2)], axis=1)
        own_k = (dk[s * ROWS : (s + 1) * ROWS, :] * SCALE).astype(BF)
        rhs = jnp.concatenate(
            [
                dq[s, 0:256, :],
                dq[s, 256:512, :],
                jnp.concatenate([dq[s, 512:640, :], own_k], axis=0),
            ],
            axis=1,
        )
        res = mm(spread, rhs)
        for t in range(3):
            dqk_out[:, s, 8 * t : 8 * t + 8, :] = (
                res[:, t * HEAD : (t + 1) * HEAD].reshape(NDP, 8, HEAD).astype(BF)
            )


def attend(lengths, slot_col, slot_row, r1, r2):
    return pl.pallas_call(
        attend_kernel,
        out_shape=(
            jax.ShapeDtypeStruct((NDP, 16, HEAD), BF),
            jax.ShapeDtypeStruct((NDP, NS, 24, HEAD), BF),
        ),
        in_specs=[SMEM, VMEM, VMEM, VMEM, VMEM],
        out_specs=(VMEM, VMEM),
        scratch_shapes=[
            pltpu.VMEM((NS, PER * ROWS, HEAD), BF),
            pltpu.VMEM((NS, PER * ROWS, HEAD), BF),
            pltpu.VMEM((GROUP, HEAD), BF),
            pltpu.VMEM((GROUP, HEAD), BF),
            pltpu.VMEM((NS, PER * ROWS, HEAD), BF),
            pltpu.VMEM((GROUP, HEAD), F32),
            pltpu.VMEM((GROUP, HEAD), F32),
        ],
        compiler_params=params(),
        cost_estimate=cost(4e9, 6e6),
        name="attend_back",
    )(lengths, slot_col, slot_row, r1, r2)


def weight_terms_kernel(slot_col_ref, r_ref, x_ref, dv_ref, out_ref):
    @pl.when(pl.program_id(0) == 0)
    def _():
        lane = lax.broadcasted_iota(jnp.int32, (GROUP, NDP * 16), 1)
        row = lax.broadcasted_iota(jnp.int32, (GROUP, NDP * 16), 0)
        hit = ((lane // 16) * CAP + lane % 4 == slot_col_ref[...]) & (
            (lane % 16) // 4 == row // ROWS
        )
        dv_ref[...] = mm(ones_where(hit), r_ref[...].reshape(NDP * 16, HEAD)).astype(BF)

    terms = mm_tn(x_ref[...], dv_ref[...]).astype(BF)
    block = out_ref.shape[3]
    for x in range(NX):
        for c in range(NC):
            at = (x * NC + c) * block
            out_ref[c, x, 0] = terms[at : at + block, :]


def weight_terms(slot_col, r, x_all):
    block = x_all.shape[1] // NDP
    return pl.pallas_call(
        weight_terms_kernel,
        grid=(NZ,),
        out_shape=(
            jax.ShapeDtypeStruct((GROUP, HEAD), BF),
            jax.ShapeDtypeStruct((NC, NX, NZ, block, HEAD), BF),
        ),
        in_specs=[
            pl.BlockSpec((GROUP, 1), lambda i: (0, 0)),
            pl.BlockSpec((NDP, 16, HEAD), lambda i: (0, 0, 0)),
            pl.BlockSpec((GROUP, NX * NC * block), lambda i: (0, i)),
        ],
        out_specs=(
            pl.BlockSpec((GROUP, HEAD), lambda i: (0, 0)),
            pl.BlockSpec((NC, NX, 1, block, HEAD), lambda i: (0, 0, i, 0, 0)),
        ),
        compiler_params=params(),
        cost_estimate=cost(0.8e9, 7e6),
        name="weight_terms",
    )(slot_col, r, x_all)


def unpack_kernel(slot_col_ref, r_ref, q_ref, k_ref):
    lane = lax.broadcasted_iota(jnp.int32, (ROWS, NDP * 8), 1)
    hit = (lane // 8) * CAP + lane % 4 == slot_col_ref[...]
    place = (lane % 8) // 4
    pick = jnp.concatenate([ones_where(hit & (place == m)) for m in range(2)], axis=0)
    for s in range(NS):
        rhs = jnp.concatenate(
            [
                r_ref[:, s, 8 * t : 8 * t + 8, :].astype(F32).reshape(NDP * 8, HEAD).astype(BF)
                for t in range(3)
            ],
            axis=1,
        )
        res = mm(pick, rhs).astype(BF)
        for m in range(PER):
            t, at = m // 2, (m % 2) * ROWS
            q_ref[:, s * QW + m * HEAD : s * QW + (m + 1) * HEAD] = res[
                at : at + ROWS, t * HEAD : (t + 1) * HEAD
            ]
        k_ref[:, s * HEAD : (s + 1) * HEAD] = res[ROWS : 2 * ROWS, 2 * HEAD : 3 * HEAD]


def unpack(slot_col, r):
    return pl.pallas_call(
        unpack_kernel,
        out_shape=(
            jax.ShapeDtypeStruct((ROWS, NS * QW), BF),
            jax.ShapeDtypeStruct((ROWS, NS * HEAD), BF),
        ),
        in_specs=[VMEM, VMEM],
        out_specs=(VMEM, VMEM),
        compiler_params=params(),
        cost_estimate=cost(0.5e9, 4e6),
        name="unpack",
    )(slot_col, r)


def dp_of(z, x, c):
    return (z * NX + x) * NC + c


EACH = [(z, x, c) for z in range(NZ) for x in range(NX) for c in range(NC)]


def along_z(value, d):
    return lax.ppermute(value, "dp", [(dp_of(z, x, c), dp_of((z + d) % NZ, x, c)) for z, x, c in EACH])


def along_x(value, d):
    return lax.ppermute(value, "dp", [(dp_of(z, x, c), dp_of(z, (x + d) % NX, c)) for z, x, c in EACH])


def along_c(value):
    return lax.ppermute(value, "dp", [(dp_of(z, x, c), dp_of(z, x, 1 - c)) for z, x, c in EACH])


def along_seq(value, d):
    return lax.ppermute(value, "seq", [(s, (s + d) % NS) for s in range(NS)])


def rank_of(label, key):
    same = (label[:, None] == label[None, :]) & (key[None, :] < key[:, None])
    return jnp.sum(same.astype(jnp.int32), axis=1)


def in_order(parts, own):
    count = len(parts)
    index = jnp.arange(count, dtype=jnp.int32).reshape((count,) + (1,) * parts[0].ndim)
    total = jnp.zeros((count,) + parts[0].shape, parts[0].dtype)
    for d, part in enumerate(parts):
        total = jnp.where(index == (own - d) % count, part[None], total)
    return total


def shards(
    x_saved, q_saved, k_saved, grad_attn, token_coef, dest_of, source_of, lengths, value_weight
):
    dp, seq = lax.axis_index("dp"), lax.axis_index("seq")
    z, x, c = dp // (NX * NC), (dp // NC) % NX, dp % NC

    z_parts = [value_weight] + [along_z(value_weight, d) for d in range(1, NZ)]

    target = dest_of // GROUP
    send_slot = target * CAP + rank_of(target, jnp.arange(ROWS, dtype=jnp.int32))
    anchor = source_of // GROUP
    recv_slot = anchor * CAP + rank_of(anchor, source_of)
    slots = jnp.stack([send_slot, recv_slot])
    coef = token_coef[:, None]

    first = pack_first(send_slot[None], coef, q_saved, k_saved, grad_attn)
    r1 = lax.all_to_all(
        first.reshape(NDP * NS, 32, HEAD), ("dp", "seq"), split_axis=0, concat_axis=0, tiled=True
    )
    all_slots = in_order([slots] + [along_seq(slots, d) for d in range(1, NS)], seq)
    send_all, recv_all = all_slots[:, 0], all_slots[:, 1]

    stage = jnp.stack(z_parts)
    x_parts = [stage] + [along_x(stage, d) for d in range(1, NX)]
    pieces = []
    for part in x_parts:
        pieces += [part, along_c(part)]
    x_all = lax.all_gather(x_saved, "seq", axis=0, tiled=True)
    values, weight = values_of(jnp.stack([z, x, c]).astype(jnp.int32), x_saved, pieces)

    second = pack_second(send_slot[None], coef, grad_attn, values)
    r2 = lax.all_to_all(
        second.reshape(NDP * NS, 16, HEAD), ("dp", "seq"), split_axis=0, concat_axis=0, tiled=True
    )

    dv_out, dqk_out = attend(
        lengths[0],
        recv_all.reshape(GROUP, 1),
        recv_all,
        r1.reshape(NDP, NS, 32, HEAD),
        r2.reshape(NDP, NS, 16, HEAD),
    )
    dv_back = lax.all_to_all(dv_out, "dp", split_axis=0, concat_axis=0, tiled=True)
    dqk_back = lax.all_to_all(
        dqk_out.reshape(NDP * NS, 24, HEAD), ("dp", "seq"), split_axis=0, concat_axis=0, tiled=True
    )

    dv_head, terms = weight_terms(send_all.reshape(GROUP, 1), dv_back, x_all)

    def pick(value, at):
        return lax.dynamic_index_in_dim(value, at, 0, keepdims=False)

    part = pick(terms, c).astype(F32) + along_c(pick(terms, 1 - c)).astype(F32)
    part = part.astype(BF)
    total = pick(part, x).astype(F32)
    for d in range(1, NX):
        total = total + along_x(pick(part, (x + d) % NX), d).astype(F32)
    part = total.astype(BF)
    total = pick(part, z).astype(F32)
    for d in range(1, NZ):
        total = total + along_z(pick(part, (z + d) % NZ), d).astype(F32)
    own = total / math.sqrt(GROUP * NDP)
    heads = in_order([own] + [along_seq(own, d) for d in range(1, NS)], seq)
    grad_v_weight = jnp.concatenate([heads[s] for s in range(NS)], axis=1)

    dv_view = dv_head.reshape(NS, ROWS, HEAD)
    dv_parts = [pick(dv_view, seq)]
    for d in range(1, NS):
        dv_parts.append(along_seq(pick(dv_view, (seq + d) % NS), d))
    dv_heads = in_order(dv_parts, seq)
    dv_src = jnp.concatenate([dv_heads[s] for s in range(NS)], axis=1)
    grad_x = mm_nt(dv_src, weight).astype(BF)

    grad_q, grad_k = unpack(send_slot[:, None], dqk_back.reshape(NDP, NS, 24, HEAD))
    return (grad_x, grad_q, grad_k, grad_v_weight)


def solution(mesh):
    rows = P(("dp", "seq"), None)
    flat = P(("dp", "seq"))
    whole = P("dp", None)
    return jax.shard_map(
        shards,
        mesh=mesh,
        in_specs=(rows, rows, rows, rows, flat, flat, flat, whole, whole),
        out_specs=(rows, rows, rows, whole),
        check_vma=False,
    )
```

```python
import functools
import math

import jax
import jax.numpy as jnp
from jax import lax
from jax.experimental import pallas as pl
from jax.experimental.pallas import tpu as pltpu
from jax.sharding import PartitionSpec as P

HEAD = 128
CAP = 4
NZ, NX, NC, NS = 8, 4, 2, 4
NDP = NZ * NX * NC
ROWS = 128
GROUP = ROWS * NS
PER = 5
QW = PER * HEAD
BF = jnp.bfloat16
F32 = jnp.float32
SCALE = HEAD ** (-0.5)
LIMIT = 58 * 1024 * 1024

VMEM = pl.BlockSpec(memory_space=pltpu.VMEM)
SMEM = pl.BlockSpec(memory_space=pltpu.SMEM)


def params():
    return pltpu.CompilerParams(vmem_limit_bytes=LIMIT)


def cost(flops, bytes_accessed):
    return pl.CostEstimate(flops=int(flops), bytes_accessed=int(bytes_accessed), transcendentals=0)


def ones_where(hit):
    return jnp.where(hit, 1.0, 0.0).astype(BF)


def mm(a, b):
    return jnp.dot(a, b, preferred_element_type=F32)


def mm_nt(a, b):
    return lax.dot_general(a, b, (((1,), (1,)), ((), ())), preferred_element_type=F32)


def mm_tn(a, b):
    return lax.dot_general(a, b, (((0,), (0,)), ((), ())), preferred_element_type=F32)


def pack_rows_kernel(slots_ref, coef_ref, q_ref, k_ref, g_ref, out_ref):
    row = lax.broadcasted_iota(jnp.int32, (256, ROWS), 0)
    hit = (pl.program_id(0) * 16 + row // 16) * CAP + row % 4 == slots_ref[...]
    place = (row % 16) // 4
    onehot = jnp.concatenate([ones_where(hit & (place == m)) for m in range(4)], axis=1)

    def chunk(s, m):
        if m < PER:
            return q_ref[:, s * QW + m * HEAD : s * QW + (m + 1) * HEAD]
        if m < 2 * PER + 1 and m > PER:
            at = s * QW + (m - PER - 1) * HEAD
            return (coef_ref[...] * g_ref[:, at : at + HEAD].astype(F32)).astype(BF)
        return k_ref[:, s * HEAD : (s + 1) * HEAD]

    for t in range(3):
        rhs = jnp.concatenate(
            [
                jnp.concatenate([chunk(s, 4 * t + m) for m in range(4)], axis=0)
                for s in range(NS)
            ],
            axis=1,
        )
        res = mm(onehot, rhs).astype(BF)
        for s in range(NS):
            out_ref[:, s, 16 * t : 16 * t + 16, :] = res[:, s * HEAD : (s + 1) * HEAD].reshape(
                16, 16, HEAD
            )


def pack_rows(slots, coef, q, k, g):
    return pl.pallas_call(
        pack_rows_kernel,
        grid=(4,),
        out_shape=jax.ShapeDtypeStruct((NDP, NS, 48, HEAD), BF),
        in_specs=[
            pl.BlockSpec((1, ROWS), lambda i: (0, 0)),
            pl.BlockSpec((ROWS, 1), lambda i: (0, 0)),
            pl.BlockSpec((ROWS, NS * QW), lambda i: (0, 0)),
            pl.BlockSpec((ROWS, NS * HEAD), lambda i: (0, 0)),
            pl.BlockSpec((ROWS, NS * QW), lambda i: (0, 0)),
        ],
        out_specs=pl.BlockSpec((16, NS, 48, HEAD), lambda i: (i, 0, 0, 0)),
        compiler_params=params(),
        cost_estimate=cost(1.6e9, 5e6),
        name="pack_rows",
    )(slots, coef, q, k, g)


def values_kernel(place_ref, slot_ref, x_ref, *refs):
    pieces, (out_ref, w_ref) = refs[: NX * NC], refs[NX * NC :]
    at_x0, at_c0 = place_ref[0], place_ref[1]
    block = w_ref.shape[0] // NDP
    for dx in range(NX):
        for dc in range(NC):
            at = lax.rem(at_x0 - dx + NX, NX) * NC + lax.rem(at_c0 + dc, NC)
            for z in range(NZ):
                start = pl.multiple_of((z * NX * NC + at) * block, 16)
                w_ref[pl.ds(start, block), :] = pieces[dx * NC + dc][z]
    row = lax.broadcasted_iota(jnp.int32, (NDP * 16, ROWS), 0)
    wanted = (row // 16) * CAP + row % 4
    of_seq = (row % 16) // 4
    value = mm(x_ref[...], w_ref[...]).astype(BF)
    spread = jnp.concatenate(
        [ones_where((wanted == slot_ref[s : s + 1, :]) & (of_seq == s)) for s in range(NS)],
        axis=1,
    )
    out_ref[...] = mm(spread, value).astype(BF).reshape(NDP, 16, HEAD)


def values_of(place, slots, x_all, pieces):
    return pl.pallas_call(
        values_kernel,
        out_shape=(
            jax.ShapeDtypeStruct((NDP, 16, HEAD), BF),
            jax.ShapeDtypeStruct((x_all.shape[1], HEAD), BF),
        ),
        in_specs=[SMEM] + [VMEM] * (2 + len(pieces)),
        out_specs=(VMEM, VMEM),
        compiler_params=params(),
        cost_estimate=cost(0.8e9, 8e6),
        name="values",
    )(place, slots, x_all, *pieces)


def turn_kernel(x_ref, out_ref):
    out_ref[...] = x_ref[...].T


def turn(x_all):
    depth = x_all.shape[1]
    width = depth // NZ
    return pl.pallas_call(
        turn_kernel,
        grid=(NZ,),
        out_shape=jax.ShapeDtypeStruct((depth, GROUP), BF),
        in_specs=[pl.BlockSpec((GROUP, width), lambda i: (0, i))],
        out_specs=pl.BlockSpec((width, GROUP), lambda i: (i, 0)),
        compiler_params=params(),
        cost_estimate=cost(1e6, 11e6),
        name="turn",
    )(x_all)


def window(s):
    return max(0, s - 2) * ROWS, (s + 1) * ROWS


def probs_kernel(
    len_ref, slot_col_ref, slot_row_ref, r_ref, v_ref, both_out, qs, ks, ds, p0, p1, p2, p3, dv
):
    for s in range(NS):
        lane = lax.broadcasted_iota(jnp.int32, (ROWS, NDP * 16), 1)
        hit = (lane // 16) * CAP + lane % 4 == slot_col_ref[s * ROWS : (s + 1) * ROWS, :]
        place = (lane % 16) // 4
        pick = jnp.concatenate([ones_where(hit & (place == m)) for m in range(4)], axis=0)
        rhs = jnp.concatenate(
            [r_ref[:, s, 16 * t : 16 * t + 16, :].reshape(NDP * 16, HEAD) for t in range(3)],
            axis=1,
        )
        res = mm(pick, rhs).astype(BF)
        qs[s, 0:512, :] = res[:, 0:128]
        qs[s, 512:640, :] = res[0:128, 128:256]
        ks[s * ROWS : (s + 1) * ROWS, :] = res[128:256, 128:256]
        ds[s, 0:256, :] = res[256:512, 128:256]
        ds[s, 256:640, :] = res[0:384, 256:384]

    first, second = len_ref[0], len_ref[0] + len_ref[1]
    dv[...] = jnp.zeros_like(dv)
    for s, p_ref in enumerate((p0, p1, p2, p3)):
        lo, hi = window(s)
        width = hi - lo
        q_pos = s * ROWS + lax.broadcasted_iota(jnp.int32, (ROWS, width), 0)
        k_pos = lo + lax.broadcasted_iota(jnp.int32, (ROWS, width), 1)
        begin = jnp.where(q_pos >= second, second, jnp.where(q_pos >= first, first, 0))
        visible = (k_pos <= q_pos) & (k_pos >= begin)
        scores = mm_nt(qs[s], ks[lo:hi, :]).reshape(PER, ROWS, width) * SCALE
        scores = jnp.where(visible[None], scores, -jnp.inf)
        weights = jnp.exp(scores - jnp.max(scores, axis=2, keepdims=True))
        probs = (weights / jnp.sum(weights, axis=2, keepdims=True)).reshape(PER * ROWS, width)
        p_ref[...] = probs
        dv[lo:hi, :] += mm_tn(probs.astype(BF), ds[s])

    row = lax.broadcasted_iota(jnp.int32, (NDP * 16, ROWS), 0)
    wanted = (row // 16) * CAP + row % 4
    of_seq = (row % 16) // 4
    spread = jnp.concatenate(
        [ones_where((wanted == slot_row_ref[s : s + 1, :]) & (of_seq == s)) for s in range(NS)],
        axis=1,
    )
    both_out[:, 0:16, :] = v_ref[...]
    both_out[:, 16:32, :] = mm(spread, dv[...].astype(BF)).astype(BF).reshape(NDP, 16, HEAD)


def probs_of(lengths, slot_col, slot_row, r, v):
    widths = [window(s)[1] - window(s)[0] for s in range(NS)]
    return pl.pallas_call(
        probs_kernel,
        out_shape=(
            jax.ShapeDtypeStruct((NDP, 32, HEAD), BF),
            jax.ShapeDtypeStruct((NS, PER * ROWS, HEAD), BF),
            jax.ShapeDtypeStruct((GROUP, HEAD), BF),
            jax.ShapeDtypeStruct((NS, PER * ROWS, HEAD), BF),
        )
        + tuple(jax.ShapeDtypeStruct((PER * ROWS, w), F32) for w in widths),
        in_specs=[SMEM, VMEM, VMEM, VMEM, VMEM],
        out_specs=(VMEM,) * 8,
        scratch_shapes=[pltpu.VMEM((GROUP, HEAD), F32)],
        compiler_params=params(),
        cost_estimate=cost(3e9, 9e6),
        name="probs",
    )(lengths, slot_col, slot_row, r, v)


def grads_kernel(
    slot_col_ref, slot_row_ref, r_ref, qs, ks, ds, p0, p1, p2, p3, dqk_out, vs, dq, dk
):
    lane = lax.broadcasted_iota(jnp.int32, (GROUP, NDP * 16), 1)
    row = lax.broadcasted_iota(jnp.int32, (GROUP, NDP * 16), 0)
    hit = ((lane // 16) * CAP + lane % 4 == slot_col_ref[...]) & ((lane % 16) // 4 == row // ROWS)
    vs[...] = mm(ones_where(hit), r_ref[:, 0:16, :].reshape(NDP * 16, HEAD)).astype(BF)
    dk[...] = jnp.zeros_like(dk)
    for s, p_ref in enumerate((p0, p1, p2, p3)):
        lo, hi = window(s)
        probs = p_ref[...]
        dprobs = mm_nt(ds[s], vs[lo:hi, :])
        delta = jnp.sum(probs.astype(BF).astype(F32) * dprobs, axis=1, keepdims=True)
        dscores = (probs * (dprobs - delta)).astype(BF)
        dq[s] = (mm(dscores, ks[lo:hi, :]) * SCALE).astype(BF)
        dk[lo:hi, :] += mm_tn(dscores, qs[s])

    row = lax.broadcasted_iota(jnp.int32, (NDP * 8, ROWS), 0)
    wanted = (row // 8) * CAP + row % 4
    place = (row % 8) // 4
    for s in range(NS):
        hit = wanted == slot_row_ref[s : s + 1, :]
        spread = jnp.concatenate([ones_where(hit & (place == m)) for m in range(2)], axis=1)
        own_k = (dk[s * ROWS : (s + 1) * ROWS, :] * SCALE).astype(BF)
        rhs = jnp.concatenate(
            [
                dq[s, 0:256, :],
                dq[s, 256:512, :],
                jnp.concatenate([dq[s, 512:640, :], own_k], axis=0),
            ],
            axis=1,
        )
        res = mm(spread, rhs)
        for t in range(3):
            dqk_out[:, s, 8 * t : 8 * t + 8, :] = (
                res[:, t * HEAD : (t + 1) * HEAD].reshape(NDP, 8, HEAD).astype(BF)
            )


def grads_of(slot_col, slot_row, r, kept):
    return pl.pallas_call(
        grads_kernel,
        out_shape=jax.ShapeDtypeStruct((NDP, NS, 24, HEAD), BF),
        in_specs=[VMEM] * (3 + len(kept)),
        out_specs=VMEM,
        scratch_shapes=[
            pltpu.VMEM((GROUP, HEAD), BF),
            pltpu.VMEM((NS, PER * ROWS, HEAD), BF),
            pltpu.VMEM((GROUP, HEAD), F32),
        ],
        compiler_params=params(),
        cost_estimate=cost(3e9, 8e6),
        name="grads",
    )(slot_col, slot_row, r, *kept)


def weight_terms_kernel(slot_col_ref, r_ref, x_ref, dv_ref, out_ref):
    @pl.when(pl.program_id(0) == 0)
    def _():
        lane = lax.broadcasted_iota(jnp.int32, (ROWS, NDP * 16), 1)
        wanted = (lane // 16) * CAP + lane % 4
        of_seq = (lane % 16) // 4
        rows = r_ref[:, 16:32, :].reshape(NDP * 16, HEAD)
        for d in range(NS):
            mine = slice(d * ROWS, (d + 1) * ROWS)
            hit = (wanted == slot_col_ref[mine, :]) & (of_seq == d)
            dv_ref[mine, :] = mm(ones_where(hit), rows).astype(BF)

    terms = mm(x_ref[...], dv_ref[...]).astype(BF)
    block = out_ref.shape[3]
    for x in range(NX):
        for c in range(NC):
            at = (x * NC + c) * block
            out_ref[c, x, 0] = terms[at : at + block, :]


def weight_terms(slot_col, r, x_turned):
    block = x_turned.shape[0] // NDP
    return pl.pallas_call(
        weight_terms_kernel,
        grid=(NZ,),
        out_shape=(
            jax.ShapeDtypeStruct((GROUP, HEAD), BF),
            jax.ShapeDtypeStruct((NC, NX, NZ, block, HEAD), BF),
        ),
        in_specs=[
            pl.BlockSpec((GROUP, 1), lambda i: (0, 0)),
            pl.BlockSpec((NDP, 32, HEAD), lambda i: (0, 0, 0)),
            pl.BlockSpec((NX * NC * block, GROUP), lambda i: (i, 0)),
        ],
        out_specs=(
            pl.BlockSpec((GROUP, HEAD), lambda i: (0, 0)),
            pl.BlockSpec((NC, NX, 1, block, HEAD), lambda i: (0, 0, i, 0, 0)),
        ),
        compiler_params=params(),
        cost_estimate=cost(0.8e9, 7e6),
        name="weight_terms",
    )(slot_col, r, x_turned)


def grad_x_kernel(dv_ref, w_ref, out_ref):
    dv = jnp.concatenate([dv_ref[s] for s in range(NS)], axis=1)
    w = jnp.concatenate([w_ref[s] for s in range(NS)], axis=1)
    out_ref[...] = mm_nt(dv, w).astype(BF)


def grad_x_of(dv, w):
    depth = w.shape[1]
    width = 1024
    return pl.pallas_call(
        grad_x_kernel,
        grid=(depth // width,),
        out_shape=jax.ShapeDtypeStruct((ROWS, depth), BF),
        in_specs=[
            pl.BlockSpec((NS, ROWS, HEAD), lambda i: (0, 0, 0)),
            pl.BlockSpec((NS, width, HEAD), lambda i: (0, i, 0)),
        ],
        out_specs=pl.BlockSpec((ROWS, width), lambda i: (0, i)),
        compiler_params=params(),
        cost_estimate=cost(0.7e9, 7e6),
        name="grad_x",
    )(dv, w)


def unpack_kernel(slot_col_ref, r_ref, q_ref, k_ref):
    lane = lax.broadcasted_iota(jnp.int32, (ROWS, NDP * 8), 1)
    hit = (lane // 8) * CAP + lane % 4 == slot_col_ref[...]
    place = (lane % 8) // 4
    pick = jnp.concatenate([ones_where(hit & (place == m)) for m in range(2)], axis=0)
    for s in range(NS):
        rhs = jnp.concatenate(
            [
                r_ref[:, s, 8 * t : 8 * t + 8, :].astype(F32).reshape(NDP * 8, HEAD).astype(BF)
                for t in range(3)
            ],
            axis=1,
        )
        res = mm(pick, rhs).astype(BF)
        for m in range(PER):
            t, at = m // 2, (m % 2) * ROWS
            q_ref[:, s * QW + m * HEAD : s * QW + (m + 1) * HEAD] = res[
                at : at + ROWS, t * HEAD : (t + 1) * HEAD
            ]
        k_ref[:, s * HEAD : (s + 1) * HEAD] = res[ROWS : 2 * ROWS, 2 * HEAD : 3 * HEAD]


def unpack(slot_col, r):
    return pl.pallas_call(
        unpack_kernel,
        out_shape=(
            jax.ShapeDtypeStruct((ROWS, NS * QW), BF),
            jax.ShapeDtypeStruct((ROWS, NS * HEAD), BF),
        ),
        in_specs=[VMEM, VMEM],
        out_specs=(VMEM, VMEM),
        compiler_params=params(),
        cost_estimate=cost(0.5e9, 4e6),
        name="unpack",
    )(slot_col, r)


def dp_of(z, x, c):
    return (z * NX + x) * NC + c


EACH = [(z, x, c) for z in range(NZ) for x in range(NX) for c in range(NC)]


def along_z(value, d):
    return lax.ppermute(value, "dp", [(dp_of(z, x, c), dp_of((z + d) % NZ, x, c)) for z, x, c in EACH])


def along_x(value, d):
    return lax.ppermute(value, "dp", [(dp_of(z, x, c), dp_of(z, (x + d) % NX, c)) for z, x, c in EACH])


def along_c(value):
    return lax.ppermute(value, "dp", [(dp_of(z, x, c), dp_of(z, x, 1 - c)) for z, x, c in EACH])


def along_seq(value, d):
    return lax.ppermute(value, "seq", [(s, (s + d) % NS) for s in range(NS)])


def rank_of(label, key):
    same = (label[:, None] == label[None, :]) & (key[None, :] < key[:, None])
    return jnp.sum(same.astype(jnp.int32), axis=1)


def in_order(parts, own):
    count = len(parts)
    index = jnp.arange(count, dtype=jnp.int32).reshape((count,) + (1,) * parts[0].ndim)
    total = jnp.zeros((count,) + parts[0].shape, parts[0].dtype)
    for d, part in enumerate(parts):
        total = jnp.where(index == (own - d) % count, part[None], total)
    return total


def shards(
    x_saved, q_saved, k_saved, grad_attn, token_coef, dest_of, source_of, lengths, value_weight
):
    dp, seq = lax.axis_index("dp"), lax.axis_index("seq")
    z, x, c = dp // (NX * NC), (dp // NC) % NX, dp % NC

    def pick(value, at):
        return lax.dynamic_index_in_dim(value, at, 0, keepdims=False)

    target = dest_of // GROUP
    send_slot = target * CAP + rank_of(target, jnp.arange(ROWS, dtype=jnp.int32))
    anchor = source_of // GROUP
    recv_slot = anchor * CAP + rank_of(anchor, source_of)
    slots = jnp.stack([send_slot, recv_slot])

    stage = lax.dynamic_slice_in_dim(value_weight, seq * HEAD, HEAD, axis=1)[None]
    for bit in (1, 2, 4):
        swap = [(dp_of(a, b, e), dp_of(a ^ bit, b, e)) for a, b, e in EACH]
        other = lax.ppermute(stage, "dp", swap)
        mine = (z // bit) % 2 == 0
        stage = jnp.concatenate(
            [jnp.where(mine, stage, other), jnp.where(mine, other, stage)], axis=0
        )

    rows = pack_rows(send_slot[None], token_coef[:, None], q_saved, k_saved, grad_attn)
    rows, slots, stage = lax.optimization_barrier((rows, slots, stage))
    arrived = lax.all_to_all(
        rows.reshape(NDP * NS, 48, HEAD), ("dp", "seq"), split_axis=0, concat_axis=0, tiled=True
    )
    slot_parts = [slots] + [along_seq(slots, d) for d in range(1, NS)]
    all_slots = in_order(slot_parts, seq)
    send_all, recv_all = all_slots[:, 0], all_slots[:, 1]
    send_col, recv_col = send_all.reshape(GROUP, 1), recv_all.reshape(GROUP, 1)
    own_col = send_slot[:, None]
    pieces = []
    for part in [stage] + [along_x(stage, d) for d in range(1, NX)]:
        pieces += [part, along_c(part)]
    x_all = lax.all_gather(x_saved, "seq", axis=0, tiled=True)
    place = jnp.stack([x, c]).astype(jnp.int32)
    v_out, head_w = values_of(place, send_all, x_all, pieces)
    w_all = lax.all_gather(head_w, "seq", axis=0, tiled=True)
    arrived, send_col, recv_col, own_col, v_out = lax.optimization_barrier(
        (arrived, send_col, recv_col, own_col, v_out)
    )

    both, *kept = probs_of(
        lengths[0], recv_col, recv_all, arrived.reshape(NDP, NS, 48, HEAD), v_out
    )

    both = lax.all_to_all(both, "dp", split_axis=0, concat_axis=0, tiled=True)
    x_turned = turn(x_all)
    both, x_turned = lax.optimization_barrier((both, x_turned))
    dqk_out = grads_of(recv_col, recv_all, both, kept)
    dqk_out, send_col = lax.optimization_barrier((dqk_out, send_col))
    dv_head, terms = weight_terms(send_col, both, x_turned)

    dqk_back = lax.all_to_all(
        dqk_out.reshape(NDP * NS, 24, HEAD), ("dp", "seq"), split_axis=0, concat_axis=0, tiled=True
    )

    part = pick(terms, c).astype(F32) + along_c(pick(terms, 1 - c)).astype(F32)
    part = part.astype(BF)
    total = pick(part, x).astype(F32)
    for d in range(1, NX):
        total = total + along_x(pick(part, (x + d) % NX), d).astype(F32)
    dv_view = dv_head.reshape(NS, ROWS, HEAD)
    dv_parts = [pick(dv_view, seq)]
    for d in range(1, NS):
        dv_parts.append(along_seq(pick(dv_view, (seq + d) % NS), d))
    grad_x = grad_x_of(in_order(dv_parts, seq), w_all.reshape(NS, -1, HEAD))

    total, grad_x, dqk_back = lax.optimization_barrier((total, grad_x, dqk_back))
    for bit in (1, 2, 4):
        half = total.astype(BF)
        count = half.shape[0]
        view = half.reshape(count // 2, 2, *half.shape[1:])
        mine = (z // bit) % 2
        swap = [
            (dp_of(a, b, e), dp_of(a ^ bit, b, e)) for a, b, e in EACH
        ]
        keep = lax.dynamic_index_in_dim(view, mine, 1, keepdims=False)
        give = lax.dynamic_index_in_dim(view, 1 - mine, 1, keepdims=False)
        total = keep.astype(F32) + lax.ppermute(give, "dp", swap).astype(F32)
    own = total[0] / math.sqrt(GROUP * NDP)
    heads = in_order([own] + [along_seq(own, d) for d in range(1, NS)], seq)
    grad_v_weight = jnp.concatenate([heads[s] for s in range(NS)], axis=1)

    grad_q, grad_k = unpack(own_col, dqk_back.reshape(NDP, NS, 24, HEAD))
    return (grad_x, grad_q, grad_k, grad_v_weight)


def solution(mesh):
    rows = P(("dp", "seq"), None)
    flat = P(("dp", "seq"))
    whole = P("dp", None)
    return jax.shard_map(
        shards,
        mesh=mesh,
        in_specs=(rows, rows, rows, rows, flat, flat, flat, whole, whole),
        out_specs=(rows, rows, rows, whole),
        check_vma=False,
    )
```

```python
import functools
import math

import jax
import jax.numpy as jnp
from jax import lax
from jax.experimental import pallas as pl
from jax.experimental.pallas import tpu as pltpu
from jax.sharding import PartitionSpec as P

HEAD = 128
CAP = 4
NZ, NX, NC, NS = 8, 4, 2, 4
NDP = NZ * NX * NC
ROWS = 128
GROUP = ROWS * NS
PER = 5
QW = PER * HEAD
BF = jnp.bfloat16
F32 = jnp.float32
SCALE = HEAD ** (-0.5)
LIMIT = 58 * 1024 * 1024
SMALL = 24 * 1024 * 1024
BIG = 62 * 1024 * 1024

VMEM = pl.BlockSpec(memory_space=pltpu.VMEM)
SMEM = pl.BlockSpec(memory_space=pltpu.SMEM)
HBM = pl.BlockSpec(memory_space=pltpu.HBM)


def params(limit=LIMIT):
    return pltpu.CompilerParams(vmem_limit_bytes=limit)


def cost(flops, bytes_accessed):
    return pl.CostEstimate(flops=int(flops), bytes_accessed=int(bytes_accessed), transcendentals=0)


def ones_where(hit):
    return jnp.where(hit, 1.0, 0.0).astype(BF)


def mm(a, b):
    return jnp.dot(a, b, preferred_element_type=F32)


def mm_nt(a, b):
    return lax.dot_general(a, b, (((1,), (1,)), ((), ())), preferred_element_type=F32)


def mm_tn(a, b):
    return lax.dot_general(a, b, (((0,), (0,)), ((), ())), preferred_element_type=F32)


def column(row):
    n = row.shape[1]
    at = lax.broadcasted_iota(jnp.int32, (n, n), 0) == lax.broadcasted_iota(jnp.int32, (n, n), 1)
    return jnp.sum(jnp.where(at, row.astype(F32), 0.0), axis=1, keepdims=True)


def slot_column(row):
    return column(row).astype(jnp.int32)


def pack_rows_kernel(slots_ref, coef_ref, q_ref, k_ref, g_ref, out_ref):
    coef = column(coef_ref[...])
    row = lax.broadcasted_iota(jnp.int32, (256, 1), 0)
    wanted = (pl.program_id(0) * 16 + row // 16) * CAP + row % 4
    place = (row % 16) // 4
    own = slots_ref[...]
    onehot = jnp.concatenate(
        [ones_where(jnp.where(place == m, wanted, -1) == own) for m in range(4)], axis=1
    )

    def chunk(s, m):
        if m < PER:
            return q_ref[:, s * QW + m * HEAD : s * QW + (m + 1) * HEAD]
        if m < 2 * PER + 1 and m > PER:
            at = s * QW + (m - PER - 1) * HEAD
            return (coef * g_ref[:, at : at + HEAD].astype(F32)).astype(BF)
        return k_ref[:, s * HEAD : (s + 1) * HEAD]

    for t in range(3):
        rhs = jnp.concatenate(
            [
                jnp.concatenate([chunk(s, 4 * t + m) for m in range(4)], axis=0)
                for s in range(NS)
            ],
            axis=1,
        )
        res = mm(onehot, rhs).astype(BF)
        for s in range(NS):
            out_ref[:, s, 16 * t : 16 * t + 16, :] = res[:, s * HEAD : (s + 1) * HEAD].reshape(
                16, 16, HEAD
            )


def pack_rows(slots, coef, q, k, g):
    return pl.pallas_call(
        pack_rows_kernel,
        grid=(4,),
        out_shape=jax.ShapeDtypeStruct((NDP, NS, 48, HEAD), BF),
        in_specs=[
            pl.BlockSpec((1, ROWS), lambda i: (0, 0)),
            pl.BlockSpec((1, ROWS), lambda i: (0, 0)),
            pl.BlockSpec((ROWS, NS * QW), lambda i: (0, 0)),
            pl.BlockSpec((ROWS, NS * HEAD), lambda i: (0, 0)),
            pl.BlockSpec((ROWS, NS * QW), lambda i: (0, 0)),
        ],
        out_specs=pl.BlockSpec((16, NS, 48, HEAD), lambda i: (i, 0, 0, 0)),
        compiler_params=params(SMALL),
        cost_estimate=cost(1.6e9, 5e6),
        name="pack_rows",
    )(slots, coef, q, k, g)


def values_kernel(place_ref, slot_ref, x_ref, *refs):
    pieces, (out_ref, w_ref) = refs[: NX * NC], refs[NX * NC :]
    block = w_ref.shape[0] // NDP
    for dx in range(NX):
        for dc in range(NC):
            at = lax.rem(place_ref[0] - dx + NX, NX) * NC + lax.rem(place_ref[1] + dc, NC)
            for held in range(NZ):
                at_z = (held % 2) * 4 + jnp.bitwise_xor(place_ref[2] % 4, held // 2)
                start = pl.multiple_of((at_z * NX * NC + at) * block, 16)
                w_ref[pl.ds(start, block), :] = pieces[dx * NC + dc][held]
    row = lax.broadcasted_iota(jnp.int32, (NDP * 16, 1), 0)
    wanted = (row // 16) * CAP + row % 4
    of_seq = (row % 16) // 4
    value = mm(x_ref[...], w_ref[...]).astype(BF)
    spread = jnp.concatenate(
        [
            ones_where(jnp.where(of_seq == s, wanted, -1) == slot_ref[s : s + 1, :])
            for s in range(NS)
        ],
        axis=1,
    )
    out_ref[...] = mm(spread, value).astype(BF).reshape(NDP, 16, HEAD)


def values_of(place, slots, x_all, pieces):
    depth = x_all.shape[1]
    return pl.pallas_call(
        values_kernel,
        out_shape=(
            jax.ShapeDtypeStruct((NDP, 16, HEAD), BF),
            jax.ShapeDtypeStruct((depth, HEAD), BF),
        ),
        in_specs=[SMEM] + [VMEM] * (2 + NX * NC),
        out_specs=(VMEM, VMEM),
        compiler_params=params(BIG),
        cost_estimate=cost(0.8e9, 8e6),
        name="values",
    )(place, slots, x_all, *pieces)


def turn_kernel(x_ref, out_ref):
    out_ref[...] = x_ref[...].T


def turn(x_all):
    depth = x_all.shape[1]
    width = depth // NZ
    return pl.pallas_call(
        turn_kernel,
        grid=(NZ,),
        out_shape=jax.ShapeDtypeStruct((depth, GROUP), BF),
        in_specs=[pl.BlockSpec((GROUP, width), lambda i: (0, i))],
        out_specs=pl.BlockSpec((width, GROUP), lambda i: (i, 0)),
        compiler_params=params(),
        cost_estimate=cost(1e6, 11e6),
        name="turn",
    )(x_all)


def window(s):
    return max(0, s - 2) * ROWS, (s + 1) * ROWS


def probs_kernel(len_ref, slot_ref, r_ref, v_ref, *refs):
    outs, (both, qs, ks, ds, p0, p1, p2, p3, dv, sems) = refs[:8], refs[8:]
    both_out, qs_out, ks_out, ds_out = outs[:4]
    copies = []

    def send(src, dst):
        copy = pltpu.make_async_copy(src, dst, sems.at[len(copies)])
        copy.start()
        copies.append(copy)

    both[:, 0:16, :] = v_ref[...]
    lane = lax.broadcasted_iota(jnp.int32, (1, NDP * 16), 1)
    wanted = (lane // 16) * CAP + lane % 4
    place = (lane % 16) // 4
    for s in range(NS):
        own = slot_column(slot_ref[s : s + 1, :])
        pick = jnp.concatenate(
            [ones_where(jnp.where(place == m, wanted, -1) == own) for m in range(4)], axis=0
        )
        rhs = jnp.concatenate(
            [r_ref[:, s, 16 * t : 16 * t + 16, :].reshape(NDP * 16, HEAD) for t in range(3)],
            axis=1,
        )
        res = mm(pick, rhs).astype(BF)
        qs[s, 0:512, :] = res[:, 0:128]
        qs[s, 512:640, :] = res[0:128, 128:256]
        ks[s * ROWS : (s + 1) * ROWS, :] = res[128:256, 128:256]
        ds[s, 0:256, :] = res[256:512, 128:256]
        ds[s, 256:640, :] = res[0:384, 256:384]
        send(qs.at[s], qs_out.at[s])
        send(ds.at[s], ds_out.at[s])
    send(ks, ks_out)

    first, second = len_ref[0], len_ref[0] + len_ref[1]
    dv[...] = jnp.zeros_like(dv)
    for s, p_ref in enumerate((p0, p1, p2, p3)):
        lo, hi = window(s)
        width = hi - lo
        q_pos = s * ROWS + lax.broadcasted_iota(jnp.int32, (ROWS, width), 0)
        k_pos = lo + lax.broadcasted_iota(jnp.int32, (ROWS, width), 1)
        begin = jnp.where(q_pos >= second, second, jnp.where(q_pos >= first, first, 0))
        visible = (k_pos <= q_pos) & (k_pos >= begin)
        scores = mm_nt(qs[s], ks[lo:hi, :]).reshape(PER, ROWS, width) * SCALE
        scores = jnp.where(visible[None], scores, -jnp.inf)
        weights = jnp.exp(scores - jnp.max(scores, axis=2, keepdims=True))
        probs = weights / jnp.sum(weights, axis=2, keepdims=True)
        half = probs.astype(BF).reshape(PER * ROWS, width)
        p_ref[...] = half
        send(p_ref, outs[4 + s])
        dv[lo:hi, :] += mm_tn(half, ds[s])

    row = lax.broadcasted_iota(jnp.int32, (NDP * 16, 1), 0)
    wanted = (row // 16) * CAP + row % 4
    of_seq = (row % 16) // 4
    spread = jnp.concatenate(
        [
            ones_where(jnp.where(of_seq == s, wanted, -1) == slot_ref[s : s + 1, :])
            for s in range(NS)
        ],
        axis=1,
    )
    both[:, 16:32, :] = mm(spread, dv[...].astype(BF)).astype(BF).reshape(NDP, 16, HEAD)
    send(both, both_out)
    for copy in copies:
        copy.wait()


def probs_of(lengths, slots, r, v):
    shapes = [
        (NDP, 32, HEAD),
        (NS, PER * ROWS, HEAD),
        (GROUP, HEAD),
        (NS, PER * ROWS, HEAD),
    ] + [(PER * ROWS, window(s)[1] - window(s)[0]) for s in range(NS)]
    return pl.pallas_call(
        probs_kernel,
        out_shape=tuple(jax.ShapeDtypeStruct(shape, BF) for shape in shapes),
        in_specs=[SMEM, VMEM, VMEM, VMEM],
        out_specs=(HBM,) * len(shapes),
        scratch_shapes=[pltpu.VMEM(shape, BF) for shape in shapes]
        + [pltpu.VMEM((GROUP, HEAD), F32), pltpu.SemaphoreType.DMA((3 * NS + 2,))],
        compiler_params=params(BIG),
        cost_estimate=cost(3e9, 9e6),
        name="probs",
    )(lengths, slots, r, v)


def grads_kernel(slot_ref, r_ref, *refs):
    kept, dqk_out, held = refs[:7], refs[7], refs[8:15]
    qs, ks, ds = held[:3]
    out, vs, dq, dk, in_sems, out_sems = refs[15:]
    arrivals = [
        pltpu.make_async_copy(kept[n], held[n], in_sems.at[n]) for n in (2, 1, 0, 3, 4, 5, 6)
    ]
    for copy in arrivals:
        copy.start()
    lane = lax.broadcasted_iota(jnp.int32, (1, NDP * 16), 1)
    wanted = (lane // 16) * CAP + lane % 4
    of_seq = (lane % 16) // 4
    pick = jnp.concatenate(
        [
            ones_where(jnp.where(of_seq == s, wanted, -1) == slot_column(slot_ref[s : s + 1, :]))
            for s in range(NS)
        ],
        axis=0,
    )
    vs[...] = mm(pick, r_ref[:, 0:16, :].reshape(NDP * 16, HEAD)).astype(BF)
    dk[...] = jnp.zeros_like(dk)
    for copy in arrivals:
        copy.wait()
    for s in range(NS):
        lo, hi = window(s)
        probs = held[3 + s][...].astype(F32)
        dprobs = mm_nt(ds[s], vs[lo:hi, :])
        delta = jnp.sum(probs * dprobs, axis=1, keepdims=True)
        dscores = (probs * (dprobs - delta)).astype(BF)
        dq[s] = (mm(dscores, ks[lo:hi, :]) * SCALE).astype(BF)
        dk[lo:hi, :] += mm_tn(dscores, qs[s])

    row = lax.broadcasted_iota(jnp.int32, (NDP * 8, 1), 0)
    wanted = (row // 8) * CAP + row % 4
    place = (row % 8) // 4
    for s in range(NS):
        own = slot_ref[s : s + 1, :]
        spread = jnp.concatenate(
            [ones_where(jnp.where(place == m, wanted, -1) == own) for m in range(2)], axis=1
        )
        own_k = (dk[s * ROWS : (s + 1) * ROWS, :] * SCALE).astype(BF)
        rhs = jnp.concatenate(
            [
                dq[s, 0:256, :],
                dq[s, 256:512, :],
                jnp.concatenate([dq[s, 512:640, :], own_k], axis=0),
            ],
            axis=1,
        )
        res = mm(spread, rhs)
        for t in range(3):
            out[s, :, 8 * t : 8 * t + 8, :] = (
                res[:, t * HEAD : (t + 1) * HEAD].reshape(NDP, 8, HEAD).astype(BF)
            )
        pltpu.make_async_copy(out.at[s], dqk_out.at[:, s], out_sems.at[s]).start()
    for s in range(NS):
        pltpu.make_async_copy(out.at[s], dqk_out.at[:, s], out_sems.at[s]).wait()


def grads_of(slots, r, kept):
    return pl.pallas_call(
        grads_kernel,
        out_shape=jax.ShapeDtypeStruct((NDP, NS, 24, HEAD), BF),
        in_specs=[VMEM] * 2 + [HBM] * len(kept),
        out_specs=HBM,
        scratch_shapes=[pltpu.VMEM(one.shape, BF) for one in kept]
        + [
            pltpu.VMEM((NS, NDP, 24, HEAD), BF),
            pltpu.VMEM((GROUP, HEAD), BF),
            pltpu.VMEM((NS, PER * ROWS, HEAD), BF),
            pltpu.VMEM((GROUP, HEAD), F32),
            pltpu.SemaphoreType.DMA((len(kept),)),
            pltpu.SemaphoreType.DMA((NS,)),
        ],
        compiler_params=params(SMALL),
        cost_estimate=cost(3e9, 8e6),
        name="grads",
    )(slots, r, *kept)


def weight_terms_kernel(slot_ref, r_ref, x_ref, dv_ref, out_ref):
    @pl.when(pl.program_id(0) == 0)
    def _():
        lane = lax.broadcasted_iota(jnp.int32, (1, NDP * 16), 1)
        wanted = (lane // 16) * CAP + lane % 4
        of_seq = (lane % 16) // 4
        pick = []
        for s in range(NS):
            own = slot_column(slot_ref[s : s + 1, :])
            pick.append(ones_where(jnp.where(of_seq == s, wanted, -1) == own))
        rows = r_ref[...].reshape(NDP * 16, HEAD)
        dv_ref[...] = mm(jnp.concatenate(pick, axis=0), rows).astype(BF)

    terms = mm(x_ref[...], dv_ref[...]).astype(BF)
    block = out_ref.shape[3]
    for z in range(out_ref.shape[2]):
        for x in range(NX):
            for c in range(NC):
                at = ((z * NX + x) * NC + c) * block
                out_ref[c, x, z] = terms[at : at + block, :]


def weight_terms(slots, r, x_turned):
    block = x_turned.shape[0] // NDP
    steps = 4
    each = NZ // steps
    return pl.pallas_call(
        weight_terms_kernel,
        grid=(steps,),
        out_shape=(
            jax.ShapeDtypeStruct((GROUP, HEAD), BF),
            jax.ShapeDtypeStruct((NC, NX, NZ, block, HEAD), BF),
        ),
        in_specs=[
            pl.BlockSpec((NS, ROWS), lambda i: (0, 0)),
            pl.BlockSpec((NDP, 16, HEAD), lambda i: (0, 1, 0)),
            pl.BlockSpec((each * NX * NC * block, GROUP), lambda i: (i, 0)),
        ],
        out_specs=(
            pl.BlockSpec((GROUP, HEAD), lambda i: (0, 0)),
            pl.BlockSpec((NC, NX, each, block, HEAD), lambda i: (0, 0, i, 0, 0)),
        ),
        compiler_params=params(),
        cost_estimate=cost(0.8e9, 7e6),
        name="weight_terms",
    )(slots, r, x_turned)


def grad_x_kernel(dv_ref, w_ref, out_ref):
    dv = jnp.concatenate([dv_ref[s] for s in range(NS)], axis=1)
    w = jnp.concatenate([w_ref[s] for s in range(NS)], axis=1)
    out_ref[...] = mm_nt(dv, w).astype(BF)


def grad_x_of(dv, w):
    depth = w.shape[1]
    width = 1024
    return pl.pallas_call(
        grad_x_kernel,
        grid=(depth // width,),
        out_shape=jax.ShapeDtypeStruct((ROWS, depth), BF),
        in_specs=[
            pl.BlockSpec((NS, ROWS, HEAD), lambda i: (0, 0, 0)),
            pl.BlockSpec((NS, width, HEAD), lambda i: (0, i, 0)),
        ],
        out_specs=pl.BlockSpec((ROWS, width), lambda i: (0, i)),
        compiler_params=params(),
        cost_estimate=cost(0.7e9, 7e6),
        name="grad_x",
    )(dv, w)


def unpack_kernel(slot_ref, r_ref, q_ref, k_ref):
    lane = lax.broadcasted_iota(jnp.int32, (1, NDP * 8), 1)
    wanted = (lane // 8) * CAP + lane % 4
    place = (lane % 8) // 4
    own = slot_column(slot_ref[...])
    pick = jnp.concatenate(
        [ones_where(jnp.where(place == m, wanted, -1) == own) for m in range(2)], axis=0
    )
    for s in range(NS):
        rhs = jnp.concatenate(
            [
                r_ref[:, s, 8 * t : 8 * t + 8, :].astype(F32).reshape(NDP * 8, HEAD).astype(BF)
                for t in range(3)
            ],
            axis=1,
        )
        res = mm(pick, rhs).astype(BF)
        for m in range(PER):
            t, at = m // 2, (m % 2) * ROWS
            q_ref[:, s * QW + m * HEAD : s * QW + (m + 1) * HEAD] = res[
                at : at + ROWS, t * HEAD : (t + 1) * HEAD
            ]
        k_ref[:, s * HEAD : (s + 1) * HEAD] = res[ROWS : 2 * ROWS, 2 * HEAD : 3 * HEAD]


def unpack(slots, r):
    return pl.pallas_call(
        unpack_kernel,
        out_shape=(
            jax.ShapeDtypeStruct((ROWS, NS * QW), BF),
            jax.ShapeDtypeStruct((ROWS, NS * HEAD), BF),
        ),
        in_specs=[VMEM, VMEM],
        out_specs=(VMEM, VMEM),
        compiler_params=params(),
        cost_estimate=cost(0.5e9, 4e6),
        name="unpack",
    )(slots, r)


def dp_of(z, x, c):
    return (z * NX + x) * NC + c


EACH = [(z, x, c) for z in range(NZ) for x in range(NX) for c in range(NC)]


def along_z(value, d):
    return lax.ppermute(value, "dp", [(dp_of(z, x, c), dp_of((z + d) % NZ, x, c)) for z, x, c in EACH])


def along_x(value, d):
    return lax.ppermute(value, "dp", [(dp_of(z, x, c), dp_of(z, (x + d) % NX, c)) for z, x, c in EACH])


def along_c(value):
    return lax.ppermute(value, "dp", [(dp_of(z, x, c), dp_of(z, x, 1 - c)) for z, x, c in EACH])


def along_seq(value, d):
    return lax.ppermute(value, "seq", [(s, (s + d) % NS) for s in range(NS)])


def rank_of(label, key):
    same = (label[:, None] == label[None, :]) & (key[None, :] < key[:, None])
    return jnp.sum(same.astype(jnp.int32), axis=1)


def in_order(parts, own):
    count = len(parts)
    index = jnp.arange(count, dtype=jnp.int32).reshape((count,) + (1,) * parts[0].ndim)
    total = jnp.zeros((count,) + parts[0].shape, parts[0].dtype)
    for d, part in enumerate(parts):
        total = jnp.where(index == (own - d) % count, part[None], total)
    return total


def shards(
    x_saved, q_saved, k_saved, grad_attn, token_coef, dest_of, source_of, lengths, value_weight
):
    dp, seq = lax.axis_index("dp"), lax.axis_index("seq")
    z, x, c = dp // (NX * NC), (dp // NC) % NX, dp % NC

    def pick(value, at):
        return lax.dynamic_index_in_dim(value, at, 0, keepdims=False)

    target = dest_of // GROUP
    send_slot = target * CAP + rank_of(target, jnp.arange(ROWS, dtype=jnp.int32))
    anchor = source_of // GROUP
    recv_slot = anchor * CAP + rank_of(anchor, source_of)
    slots = jnp.stack([send_slot, recv_slot])

    def across_z(value, bits):
        swap = [(dp_of(a, b, e), dp_of(a ^ bits, b, e)) for a, b, e in EACH]
        return lax.ppermute(value, "dp", swap)

    own_w = lax.dynamic_slice_in_dim(value_weight, seq * HEAD, HEAD, axis=1)
    far_w = across_z(own_w, 4)
    low = z < 4
    stage = jnp.stack([jnp.where(low, own_w, far_w), jnp.where(low, far_w, own_w)])
    stage = jnp.concatenate([stage] + [across_z(stage, bits) for bits in (1, 2, 3)], axis=0)

    own_slot = send_slot[None]
    rows = pack_rows(own_slot, token_coef[None], q_saved, k_saved, grad_attn)
    rows, slots, stage = lax.optimization_barrier((rows, slots, stage))
    arrived = lax.all_to_all(
        rows.reshape(NDP * NS, 48, HEAD), ("dp", "seq"), split_axis=0, concat_axis=0, tiled=True
    )

    all_slots = in_order([slots] + [along_seq(slots, d) for d in range(1, NS)], seq)
    send_all, recv_all = all_slots[:, 0], all_slots[:, 1]
    x_all = lax.all_gather(x_saved, "seq", axis=0, tiled=True)

    pieces = []
    for part in [stage] + [along_x(stage, d) for d in range(1, NX)]:
        pieces += [part, along_c(part)]
    place = jnp.stack([x, c, z]).astype(jnp.int32)
    v_out, head_w = values_of(place, send_all, x_all, pieces)
    w_all = lax.all_gather(head_w, "seq", axis=0, tiled=True)

    arrived, recv_all, v_out = lax.optimization_barrier((arrived, recv_all, v_out))
    both, *kept = probs_of(lengths[0], recv_all, arrived.reshape(NDP, NS, 48, HEAD), v_out)
    both = lax.all_to_all(both, "dp", split_axis=0, concat_axis=0, tiled=True)
    x_turned = turn(x_all)
    both, x_turned = lax.optimization_barrier((both, x_turned))
    dqk_out = grads_of(recv_all, both, kept)
    dqk_out, send_all = lax.optimization_barrier((dqk_out, send_all))
    dv_head, terms = weight_terms(send_all, both, x_turned)

    dqk_back = lax.all_to_all(
        dqk_out.reshape(NDP * NS, 24, HEAD), ("dp", "seq"), split_axis=0, concat_axis=0, tiled=True
    )

    part = pick(terms, c).astype(F32) + along_c(pick(terms, 1 - c)).astype(F32)
    part = part.astype(BF)
    total = pick(part, x).astype(F32)
    for d in range(1, NX):
        total = total + along_x(pick(part, (x + d) % NX), d).astype(F32)
    dv_view = dv_head.reshape(NS, ROWS, HEAD)
    dv_parts = [pick(dv_view, seq)]
    for d in range(1, NS):
        dv_parts.append(along_seq(pick(dv_view, (seq + d) % NS), d))
    grad_x = grad_x_of(in_order(dv_parts, seq), w_all.reshape(NS, -1, HEAD))

    total, grad_x, dqk_back = lax.optimization_barrier((total, grad_x, dqk_back))
    half = total.astype(BF).reshape(NZ // 2, 2, *total.shape[1:])
    keep = lax.dynamic_index_in_dim(half, z % 2, 1, keepdims=False)
    give = lax.dynamic_index_in_dim(half, 1 - z % 2, 1, keepdims=False)
    half = (keep.astype(F32) + across_z(give, 1).astype(F32)).astype(BF)
    total = pick(half, z // 2).astype(F32)
    for bits in (1, 2, 3):
        total = total + across_z(pick(half, (z // 2) ^ bits), 2 * bits).astype(F32)
    own = total / math.sqrt(GROUP * NDP)
    heads = in_order([own] + [along_seq(own, d) for d in range(1, NS)], seq)
    grad_v_weight = jnp.concatenate([heads[s] for s in range(NS)], axis=1)

    grad_q, grad_k = unpack(own_slot, dqk_back.reshape(NDP, NS, 24, HEAD))
    return (grad_x, grad_q, grad_k, grad_v_weight)


def solution(mesh):
    rows = P(("dp", "seq"), None)
    flat = P(("dp", "seq"))
    whole = P("dp", None)
    return jax.shard_map(
        shards,
        mesh=mesh,
        in_specs=(rows, rows, rows, rows, flat, flat, flat, whole, whole),
        out_specs=(rows, rows, rows, whole),
        check_vma=False,
    )
```

```python
import functools
import math

import jax
import jax.numpy as jnp
from jax import lax
from jax.experimental import pallas as pl
from jax.experimental.pallas import tpu as pltpu
from jax.sharding import PartitionSpec as P

HEAD = 128
CAP = 4
NZ, NX, NC, NS = 8, 4, 2, 4
NDP = NZ * NX * NC
ROWS = 128
GROUP = ROWS * NS
PER = 5
QW = PER * HEAD
BF = jnp.bfloat16
F32 = jnp.float32
SCALE = HEAD ** (-0.5)
LIMIT = 58 * 1024 * 1024
SMALL = 24 * 1024 * 1024
BIG = 62 * 1024 * 1024

VMEM = pl.BlockSpec(memory_space=pltpu.VMEM)
SMEM = pl.BlockSpec(memory_space=pltpu.SMEM)
HBM = pl.BlockSpec(memory_space=pltpu.HBM)


def params(limit=LIMIT):
    return pltpu.CompilerParams(vmem_limit_bytes=limit)


def cost(flops, bytes_accessed):
    return pl.CostEstimate(flops=int(flops), bytes_accessed=int(bytes_accessed), transcendentals=0)


def ones_where(hit):
    return jnp.where(hit, 1.0, 0.0).astype(BF)


def mm(a, b):
    return jnp.dot(a, b, preferred_element_type=F32)


def mm_nt(a, b):
    return lax.dot_general(a, b, (((1,), (1,)), ((), ())), preferred_element_type=F32)


def mm_tn(a, b):
    return lax.dot_general(a, b, (((0,), (0,)), ((), ())), preferred_element_type=F32)


def column(row):
    n = row.shape[1]
    at = lax.broadcasted_iota(jnp.int32, (n, n), 0) == lax.broadcasted_iota(jnp.int32, (n, n), 1)
    return jnp.sum(jnp.where(at, row.astype(F32), 0.0), axis=1, keepdims=True)


def slot_column(row):
    return column(row).astype(jnp.int32)


def pack_rows_kernel(slots_ref, coef_ref, q_ref, k_ref, g_ref, out_ref):
    coef = column(coef_ref[...])
    row = lax.broadcasted_iota(jnp.int32, (256, 1), 0)
    wanted = (pl.program_id(0) * 16 + row // 16) * CAP + row % 4
    place = (row % 16) // 4
    own = slots_ref[...]
    onehot = jnp.concatenate(
        [ones_where(jnp.where(place == m, wanted, -1) == own) for m in range(4)], axis=1
    )

    def chunk(s, m):
        if m < PER:
            return q_ref[:, s * QW + m * HEAD : s * QW + (m + 1) * HEAD]
        if m == PER:
            return k_ref[:, s * HEAD : (s + 1) * HEAD]
        at = s * QW + (m - PER - 1) * HEAD
        return (coef * g_ref[:, at : at + HEAD].astype(F32)).astype(BF)

    flat = out_ref.reshape(16, NS, 44, HEAD)
    for begin in (0, 4, 7):
        rhs = jnp.concatenate(
            [
                jnp.concatenate([chunk(s, begin + m) for m in range(4)], axis=0)
                for s in range(NS)
            ],
            axis=1,
        )
        res = mm(onehot, rhs).astype(BF)
        for s in range(NS):
            flat[:, s, 4 * begin : 4 * begin + 16, :] = res[:, s * HEAD : (s + 1) * HEAD].reshape(
                16, 16, HEAD
            )


def pack_rows(slots, coef, q, k, g):
    return pl.pallas_call(
        pack_rows_kernel,
        grid=(4,),
        out_shape=jax.ShapeDtypeStruct((NDP, NS, 11, CAP, HEAD), BF),
        in_specs=[
            pl.BlockSpec((1, ROWS), lambda i: (0, 0)),
            pl.BlockSpec((1, ROWS), lambda i: (0, 0)),
            pl.BlockSpec((ROWS, NS * QW), lambda i: (0, 0)),
            pl.BlockSpec((ROWS, NS * HEAD), lambda i: (0, 0)),
            pl.BlockSpec((ROWS, NS * QW), lambda i: (0, 0)),
        ],
        out_specs=pl.BlockSpec((16, NS, 11, CAP, HEAD), lambda i: (i, 0, 0, 0, 0)),
        compiler_params=params(SMALL),
        cost_estimate=cost(1.6e9, 5e6),
        name="pack_rows",
    )(slots, coef, q, k, g)


def values_kernel(place_ref, slot_ref, x_ref, *refs):
    pieces, (out_ref, w_ref) = refs[: NX * NC], refs[NX * NC :]
    block = w_ref.shape[0] // NDP
    for dx in range(NX):
        for dc in range(NC):
            at = lax.rem(place_ref[0] - dx + NX, NX) * NC + lax.rem(place_ref[1] + dc, NC)
            for held in range(NZ):
                at_z = (held % 2) * 4 + jnp.bitwise_xor(place_ref[2] % 4, held // 2)
                start = pl.multiple_of((at_z * NX * NC + at) * block, 16)
                w_ref[pl.ds(start, block), :] = pieces[dx * NC + dc][held]
    row = lax.broadcasted_iota(jnp.int32, (NDP * 16, 1), 0)
    wanted = (row // 16) * CAP + row % 4
    of_seq = (row % 16) // 4
    value = mm(x_ref[...], w_ref[...]).astype(BF)
    spread = jnp.concatenate(
        [
            ones_where(jnp.where(of_seq == s, wanted, -1) == slot_ref[s : s + 1, :])
            for s in range(NS)
        ],
        axis=1,
    )
    out_ref[...] = mm(spread, value).astype(BF).reshape(NDP, 16, HEAD)


def values_of(place, slots, x_all, pieces):
    depth = x_all.shape[1]
    return pl.pallas_call(
        values_kernel,
        out_shape=(
            jax.ShapeDtypeStruct((NDP, 16, HEAD), BF),
            jax.ShapeDtypeStruct((depth, HEAD), BF),
        ),
        in_specs=[SMEM] + [VMEM] * (2 + NX * NC),
        out_specs=(VMEM, VMEM),
        compiler_params=params(BIG),
        cost_estimate=cost(0.8e9, 8e6),
        name="values",
    )(place, slots, x_all, *pieces)


def turn_kernel(x_ref, out_ref):
    out_ref[...] = x_ref[...].T


def turn(x_all):
    depth = x_all.shape[1]
    width = depth // NZ
    return pl.pallas_call(
        turn_kernel,
        grid=(NZ,),
        out_shape=jax.ShapeDtypeStruct((depth, GROUP), BF),
        in_specs=[pl.BlockSpec((GROUP, width), lambda i: (0, i))],
        out_specs=pl.BlockSpec((width, GROUP), lambda i: (i, 0)),
        compiler_params=params(),
        cost_estimate=cost(1e6, 11e6),
        name="turn",
    )(x_all)


def window(s):
    return max(0, s - 2) * ROWS, (s + 1) * ROWS


def probs_kernel(len_ref, slot_ref, r_ref, v_ref, *refs):
    outs, (both, qs, ks, ds, p0, p1, p2, p3, dv, sems) = refs[:8], refs[8:]
    both_out, qs_out, ks_out, ds_out = outs[:4]
    copies = []

    def send(src, dst):
        copy = pltpu.make_async_copy(src, dst, sems.at[len(copies)])
        copy.start()
        copies.append(copy)

    both[:, 0:16, :] = v_ref[...]
    lane = lax.broadcasted_iota(jnp.int32, (1, NDP * 16), 1)
    wanted = (lane // 16) * CAP + lane % 4
    place = (lane % 16) // 4
    flat = r_ref.reshape(NDP, NS, 44, HEAD)
    for s in range(NS):
        own = slot_column(slot_ref[s : s + 1, :])
        pick = jnp.concatenate(
            [ones_where(jnp.where(place == m, wanted, -1) == own) for m in range(4)], axis=0
        )
        rhs = jnp.concatenate(
            [flat[:, s, 4 * b : 4 * b + 16, :].reshape(NDP * 16, HEAD) for b in (0, 4, 7)],
            axis=1,
        )
        res = mm(pick, rhs).astype(BF)
        qs[s, 0:512, :] = res[:, 0:128]
        qs[s, 512:640, :] = res[0:128, 128:256]
        ks[s * ROWS : (s + 1) * ROWS, :] = res[128:256, 128:256]
        ds[s, 0:256, :] = res[256:512, 128:256]
        ds[s, 256:640, :] = res[128:512, 256:384]
        send(qs.at[s], qs_out.at[s])
        send(ds.at[s], ds_out.at[s])
    send(ks, ks_out)

    first, second = len_ref[0], len_ref[0] + len_ref[1]
    dv[...] = jnp.zeros_like(dv)
    for s, p_ref in enumerate((p0, p1, p2, p3)):
        lo, hi = window(s)
        width = hi - lo
        q_pos = s * ROWS + lax.broadcasted_iota(jnp.int32, (ROWS, width), 0)
        k_pos = lo + lax.broadcasted_iota(jnp.int32, (ROWS, width), 1)
        begin = jnp.where(q_pos >= second, second, jnp.where(q_pos >= first, first, 0))
        visible = (k_pos <= q_pos) & (k_pos >= begin)
        scores = mm_nt(qs[s], ks[lo:hi, :]).reshape(PER, ROWS, width) * SCALE
        scores = jnp.where(visible[None], scores, -jnp.inf)
        weights = jnp.exp(scores - jnp.max(scores, axis=2, keepdims=True))
        probs = weights / jnp.sum(weights, axis=2, keepdims=True)
        half = probs.astype(BF).reshape(PER * ROWS, width)
        p_ref[...] = half
        send(p_ref, outs[4 + s])
        dv[lo:hi, :] += mm_tn(half, ds[s])

    row = lax.broadcasted_iota(jnp.int32, (NDP * 16, 1), 0)
    wanted = (row // 16) * CAP + row % 4
    of_seq = (row % 16) // 4
    spread = jnp.concatenate(
        [
            ones_where(jnp.where(of_seq == s, wanted, -1) == slot_ref[s : s + 1, :])
            for s in range(NS)
        ],
        axis=1,
    )
    both[:, 16:32, :] = mm(spread, dv[...].astype(BF)).astype(BF).reshape(NDP, 16, HEAD)
    send(both, both_out)
    for copy in copies:
        copy.wait()


def probs_of(lengths, slots, r, v):
    shapes = [
        (NDP, 32, HEAD),
        (NS, PER * ROWS, HEAD),
        (GROUP, HEAD),
        (NS, PER * ROWS, HEAD),
    ] + [(PER * ROWS, window(s)[1] - window(s)[0]) for s in range(NS)]
    return pl.pallas_call(
        probs_kernel,
        out_shape=tuple(jax.ShapeDtypeStruct(shape, BF) for shape in shapes),
        in_specs=[SMEM, VMEM, VMEM, VMEM],
        out_specs=(HBM,) * len(shapes),
        scratch_shapes=[pltpu.VMEM(shape, BF) for shape in shapes]
        + [pltpu.VMEM((GROUP, HEAD), F32), pltpu.SemaphoreType.DMA((3 * NS + 2,))],
        compiler_params=params(BIG),
        cost_estimate=cost(3e9, 9e6),
        name="probs",
    )(lengths, slots, r, v)


def grads_kernel(slot_ref, r_ref, *refs):
    kept, dqk_out, held = refs[:7], refs[7], refs[8:15]
    qs, ks, ds = held[:3]
    out, vs, dq, dk, in_sems, out_sems = refs[15:]
    arrivals = [
        pltpu.make_async_copy(kept[n], held[n], in_sems.at[n]) for n in (2, 1, 0, 3, 4, 5, 6)
    ]
    for copy in arrivals:
        copy.start()
    lane = lax.broadcasted_iota(jnp.int32, (1, NDP * 16), 1)
    wanted = (lane // 16) * CAP + lane % 4
    of_seq = (lane % 16) // 4
    pick = jnp.concatenate(
        [
            ones_where(jnp.where(of_seq == s, wanted, -1) == slot_column(slot_ref[s : s + 1, :]))
            for s in range(NS)
        ],
        axis=0,
    )
    vs[...] = mm(pick, r_ref[:, 0:16, :].reshape(NDP * 16, HEAD)).astype(BF)
    dk[...] = jnp.zeros_like(dk)
    for copy in arrivals:
        copy.wait()
    for s in range(NS):
        lo, hi = window(s)
        probs = held[3 + s][...].astype(F32)
        dprobs = mm_nt(ds[s], vs[lo:hi, :])
        delta = jnp.sum(probs * dprobs, axis=1, keepdims=True)
        dscores = (probs * (dprobs - delta)).astype(BF)
        dq[s] = (mm(dscores, ks[lo:hi, :]) * SCALE).astype(BF)
        dk[lo:hi, :] += mm_tn(dscores, qs[s])

    row = lax.broadcasted_iota(jnp.int32, (NDP * 8, 1), 0)
    wanted = (row // 8) * CAP + row % 4
    place = (row % 8) // 4
    for s in range(NS):
        own = slot_ref[s : s + 1, :]
        spread = jnp.concatenate(
            [ones_where(jnp.where(place == m, wanted, -1) == own) for m in range(2)], axis=1
        )
        own_k = (dk[s * ROWS : (s + 1) * ROWS, :] * SCALE).astype(BF)
        rhs = jnp.concatenate(
            [
                dq[s, 0:256, :],
                dq[s, 256:512, :],
                jnp.concatenate([dq[s, 512:640, :], own_k], axis=0),
            ],
            axis=1,
        )
        res = mm(spread, rhs)
        for t in range(3):
            out[s, :, 8 * t : 8 * t + 8, :] = (
                res[:, t * HEAD : (t + 1) * HEAD].reshape(NDP, 8, HEAD).astype(BF)
            )
        pltpu.make_async_copy(out.at[s], dqk_out.at[:, s], out_sems.at[s]).start()
    for s in range(NS):
        pltpu.make_async_copy(out.at[s], dqk_out.at[:, s], out_sems.at[s]).wait()


def grads_of(slots, r, kept):
    return pl.pallas_call(
        grads_kernel,
        out_shape=jax.ShapeDtypeStruct((NDP, NS, 24, HEAD), BF),
        in_specs=[VMEM] * 2 + [HBM] * len(kept),
        out_specs=HBM,
        scratch_shapes=[pltpu.VMEM(one.shape, BF) for one in kept]
        + [
            pltpu.VMEM((NS, NDP, 24, HEAD), BF),
            pltpu.VMEM((GROUP, HEAD), BF),
            pltpu.VMEM((NS, PER * ROWS, HEAD), BF),
            pltpu.VMEM((GROUP, HEAD), F32),
            pltpu.SemaphoreType.DMA((len(kept),)),
            pltpu.SemaphoreType.DMA((NS,)),
        ],
        compiler_params=params(SMALL),
        cost_estimate=cost(3e9, 8e6),
        name="grads",
    )(slots, r, *kept)


def weight_terms_kernel(slot_ref, r_ref, x_ref, dv_ref, out_ref):
    @pl.when(pl.program_id(0) == 0)
    def _():
        lane = lax.broadcasted_iota(jnp.int32, (1, NDP * 16), 1)
        wanted = (lane // 16) * CAP + lane % 4
        of_seq = (lane % 16) // 4
        pick = []
        for s in range(NS):
            own = slot_column(slot_ref[s : s + 1, :])
            pick.append(ones_where(jnp.where(of_seq == s, wanted, -1) == own))
        rows = r_ref[...].reshape(NDP * 16, HEAD)
        dv_ref[...] = mm(jnp.concatenate(pick, axis=0), rows).astype(BF)

    terms = mm(x_ref[...], dv_ref[...]).astype(BF)
    block = out_ref.shape[3]
    for z in range(out_ref.shape[2]):
        for x in range(NX):
            for c in range(NC):
                at = ((z * NX + x) * NC + c) * block
                out_ref[c, x, z] = terms[at : at + block, :]


def weight_terms(slots, r, x_turned):
    block = x_turned.shape[0] // NDP
    steps = 4
    each = NZ // steps
    return pl.pallas_call(
        weight_terms_kernel,
        grid=(steps,),
        out_shape=(
            jax.ShapeDtypeStruct((GROUP, HEAD), BF),
            jax.ShapeDtypeStruct((NC, NX, NZ, block, HEAD), BF),
        ),
        in_specs=[
            pl.BlockSpec((NS, ROWS), lambda i: (0, 0)),
            pl.BlockSpec((NDP, 16, HEAD), lambda i: (0, 1, 0)),
            pl.BlockSpec((each * NX * NC * block, GROUP), lambda i: (i, 0)),
        ],
        out_specs=(
            pl.BlockSpec((GROUP, HEAD), lambda i: (0, 0)),
            pl.BlockSpec((NC, NX, each, block, HEAD), lambda i: (0, 0, i, 0, 0)),
        ),
        compiler_params=params(),
        cost_estimate=cost(0.8e9, 7e6),
        name="weight_terms",
    )(slots, r, x_turned)


def grad_x_kernel(dv_ref, w_ref, out_ref):
    dv = jnp.concatenate([dv_ref[s] for s in range(NS)], axis=1)
    w = jnp.concatenate([w_ref[s] for s in range(NS)], axis=1)
    out_ref[...] = mm_nt(dv, w).astype(BF)


def grad_x_of(dv, w):
    depth = w.shape[1]
    width = 1024
    return pl.pallas_call(
        grad_x_kernel,
        grid=(depth // width,),
        out_shape=jax.ShapeDtypeStruct((ROWS, depth), BF),
        in_specs=[
            pl.BlockSpec((NS, ROWS, HEAD), lambda i: (0, 0, 0)),
            pl.BlockSpec((NS, width, HEAD), lambda i: (0, i, 0)),
        ],
        out_specs=pl.BlockSpec((ROWS, width), lambda i: (0, i)),
        compiler_params=params(),
        cost_estimate=cost(0.7e9, 7e6),
        name="grad_x",
    )(dv, w)


def unpack_kernel(slot_ref, r_ref, q_ref, k_ref):
    lane = lax.broadcasted_iota(jnp.int32, (1, NDP * 8), 1)
    wanted = (lane // 8) * CAP + lane % 4
    place = (lane % 8) // 4
    own = slot_column(slot_ref[...])
    pick = jnp.concatenate(
        [ones_where(jnp.where(place == m, wanted, -1) == own) for m in range(2)], axis=0
    )
    for s in range(NS):
        rhs = jnp.concatenate(
            [
                r_ref[:, s, 8 * t : 8 * t + 8, :].astype(F32).reshape(NDP * 8, HEAD).astype(BF)
                for t in range(3)
            ],
            axis=1,
        )
        res = mm(pick, rhs).astype(BF)
        for m in range(PER):
            t, at = m // 2, (m % 2) * ROWS
            q_ref[:, s * QW + m * HEAD : s * QW + (m + 1) * HEAD] = res[
                at : at + ROWS, t * HEAD : (t + 1) * HEAD
            ]
        k_ref[:, s * HEAD : (s + 1) * HEAD] = res[ROWS : 2 * ROWS, 2 * HEAD : 3 * HEAD]


def unpack(slots, r):
    return pl.pallas_call(
        unpack_kernel,
        out_shape=(
            jax.ShapeDtypeStruct((ROWS, NS * QW), BF),
            jax.ShapeDtypeStruct((ROWS, NS * HEAD), BF),
        ),
        in_specs=[VMEM, VMEM],
        out_specs=(VMEM, VMEM),
        compiler_params=params(),
        cost_estimate=cost(0.5e9, 4e6),
        name="unpack",
    )(slots, r)


def dp_of(z, x, c):
    return (z * NX + x) * NC + c


EACH = [(z, x, c) for z in range(NZ) for x in range(NX) for c in range(NC)]


def along_z(value, d):
    return lax.ppermute(value, "dp", [(dp_of(z, x, c), dp_of((z + d) % NZ, x, c)) for z, x, c in EACH])


def along_x(value, d):
    return lax.ppermute(value, "dp", [(dp_of(z, x, c), dp_of(z, (x + d) % NX, c)) for z, x, c in EACH])


def along_c(value):
    return lax.ppermute(value, "dp", [(dp_of(z, x, c), dp_of(z, x, 1 - c)) for z, x, c in EACH])


def along_seq(value, d):
    return lax.ppermute(value, "seq", [(s, (s + d) % NS) for s in range(NS)])


def rank_of(label, key):
    same = (label[:, None] == label[None, :]) & (key[None, :] < key[:, None])
    return jnp.sum(same.astype(jnp.int32), axis=1)


def in_order(parts, own):
    count = len(parts)
    index = jnp.arange(count, dtype=jnp.int32).reshape((count,) + (1,) * parts[0].ndim)
    total = jnp.zeros((count,) + parts[0].shape, parts[0].dtype)
    for d, part in enumerate(parts):
        total = jnp.where(index == (own - d) % count, part[None], total)
    return total


def shards(
    x_saved, q_saved, k_saved, grad_attn, token_coef, dest_of, source_of, lengths, value_weight
):
    dp, seq = lax.axis_index("dp"), lax.axis_index("seq")
    z, x, c = dp // (NX * NC), (dp // NC) % NX, dp % NC

    def pick(value, at):
        return lax.dynamic_index_in_dim(value, at, 0, keepdims=False)

    target = dest_of // GROUP
    send_slot = target * CAP + rank_of(target, jnp.arange(ROWS, dtype=jnp.int32))
    anchor = source_of // GROUP
    recv_slot = anchor * CAP + rank_of(anchor, source_of)
    slots = jnp.stack([send_slot, recv_slot])

    def across_z(value, bits):
        swap = [(dp_of(a, b, e), dp_of(a ^ bits, b, e)) for a, b, e in EACH]
        return lax.ppermute(value, "dp", swap)

    own_w = lax.dynamic_slice_in_dim(value_weight, seq * HEAD, HEAD, axis=1)
    far_w = across_z(own_w, 4)
    low = z < 4
    stage = jnp.stack([jnp.where(low, own_w, far_w), jnp.where(low, far_w, own_w)])
    stage = jnp.concatenate([stage] + [across_z(stage, bits) for bits in (1, 2, 3)], axis=0)

    own_slot = send_slot[None]
    rows = pack_rows(own_slot, token_coef[None], q_saved, k_saved, grad_attn)
    rows, slots, stage = lax.optimization_barrier((rows, slots, stage))
    arrived = lax.all_to_all(
        rows.reshape(NDP * NS, 11, CAP, HEAD), ("dp", "seq"), split_axis=0, concat_axis=0, tiled=True
    )

    all_slots = in_order([slots] + [along_seq(slots, d) for d in range(1, NS)], seq)
    send_all, recv_all = all_slots[:, 0], all_slots[:, 1]
    x_all = lax.all_gather(x_saved, "seq", axis=0, tiled=True)

    pieces = []
    for part in [stage] + [along_x(stage, d) for d in range(1, NX)]:
        pieces += [part, along_c(part)]
    place = jnp.stack([x, c, z]).astype(jnp.int32)
    v_out, head_w = values_of(place, send_all, x_all, pieces)
    w_all = lax.all_gather(head_w, "seq", axis=0, tiled=True)

    arrived, recv_all, v_out = lax.optimization_barrier((arrived, recv_all, v_out))
    both, *kept = probs_of(lengths[0], recv_all, arrived.reshape(NDP, NS, 11, CAP, HEAD), v_out)
    both = lax.all_to_all(both, "dp", split_axis=0, concat_axis=0, tiled=True)
    x_turned = turn(x_all)
    both, x_turned = lax.optimization_barrier((both, x_turned))
    dqk_out = grads_of(recv_all, both, kept)
    dqk_out, send_all = lax.optimization_barrier((dqk_out, send_all))
    dv_head, terms = weight_terms(send_all, both, x_turned)

    dqk_back = lax.all_to_all(
        dqk_out.reshape(NDP * NS, 24, HEAD), ("dp", "seq"), split_axis=0, concat_axis=0, tiled=True
    )

    part = pick(terms, c).astype(F32) + along_c(pick(terms, 1 - c)).astype(F32)
    part = part.astype(BF)
    total = pick(part, x).astype(F32)
    for d in range(1, NX):
        total = total + along_x(pick(part, (x + d) % NX), d).astype(F32)
    dv_view = dv_head.reshape(NS, ROWS, HEAD)
    dv_parts = [pick(dv_view, seq)]
    for d in range(1, NS):
        dv_parts.append(along_seq(pick(dv_view, (seq + d) % NS), d))
    grad_x = grad_x_of(in_order(dv_parts, seq), w_all.reshape(NS, -1, HEAD))

    total, grad_x, dqk_back = lax.optimization_barrier((total, grad_x, dqk_back))
    half = total.astype(BF).reshape(NZ // 2, 2, *total.shape[1:])
    keep = lax.dynamic_index_in_dim(half, z % 2, 1, keepdims=False)
    give = lax.dynamic_index_in_dim(half, 1 - z % 2, 1, keepdims=False)
    half = (keep.astype(F32) + across_z(give, 1).astype(F32)).astype(BF)
    total = pick(half, z // 2).astype(F32)
    for bits in (1, 2, 3):
        total = total + across_z(pick(half, (z // 2) ^ bits), 2 * bits).astype(F32)
    own = total / math.sqrt(GROUP * NDP)
    grad_q, grad_k = unpack(own_slot, dqk_back.reshape(NDP, NS, 24, HEAD))
    own, grad_q, grad_k = lax.optimization_barrier((own, grad_q, grad_k))
    heads = in_order([own] + [along_seq(own, d) for d in range(1, NS)], seq)
    grad_v_weight = jnp.concatenate([heads[s] for s in range(NS)], axis=1)

    return (grad_x, grad_q, grad_k, grad_v_weight)


def solution(mesh):
    rows = P(("dp", "seq"), None)
    flat = P(("dp", "seq"))
    whole = P("dp", None)
    return jax.shard_map(
        shards,
        mesh=mesh,
        in_specs=(rows, rows, rows, rows, flat, flat, flat, whole, whole),
        out_specs=(rows, rows, rows, whole),
        check_vma=False,
    )
```

```python
import functools
import math

import jax
import jax.numpy as jnp
from jax import lax
from jax.experimental import pallas as pl
from jax.experimental.pallas import tpu as pltpu
from jax.sharding import PartitionSpec as P

HEAD = 128
CAP = 4
NZ, NX, NC, NS = 8, 4, 2, 4
NDP = NZ * NX * NC
ROWS = 128
GROUP = ROWS * NS
PER = 5
QW = PER * HEAD
BF = jnp.bfloat16
F32 = jnp.float32
SCALE = HEAD ** (-0.5)
LIMIT = 58 * 1024 * 1024
SMALL = 24 * 1024 * 1024
BIG = 62 * 1024 * 1024

VMEM = pl.BlockSpec(memory_space=pltpu.VMEM)
SMEM = pl.BlockSpec(memory_space=pltpu.SMEM)
HBM = pl.BlockSpec(memory_space=pltpu.HBM)


def params(limit=LIMIT):
    return pltpu.CompilerParams(vmem_limit_bytes=limit)


def cost(flops, bytes_accessed):
    return pl.CostEstimate(flops=int(flops), bytes_accessed=int(bytes_accessed), transcendentals=0)


def ones_where(hit):
    return jnp.where(hit, 1.0, 0.0).astype(BF)


def mm(a, b):
    return jnp.dot(a, b, preferred_element_type=F32)


def mm_nt(a, b):
    return lax.dot_general(a, b, (((1,), (1,)), ((), ())), preferred_element_type=F32)


def mm_tn(a, b):
    return lax.dot_general(a, b, (((0,), (0,)), ((), ())), preferred_element_type=F32)


def column(row):
    n = row.shape[1]
    at = lax.broadcasted_iota(jnp.int32, (n, n), 0) == lax.broadcasted_iota(jnp.int32, (n, n), 1)
    return jnp.sum(jnp.where(at, row.astype(F32), 0.0), axis=1, keepdims=True)


def slot_column(row):
    return column(row).astype(jnp.int32)


def pack_rows_kernel(slots_ref, coef_ref, q_ref, k_ref, g_ref, out_ref):
    coef = column(coef_ref[...])
    row = lax.broadcasted_iota(jnp.int32, (256, 1), 0)
    wanted = (pl.program_id(0) * 16 + row // 16) * CAP + row % 4
    place = (row % 16) // 4
    own = slots_ref[...]
    onehot = jnp.concatenate(
        [ones_where(jnp.where(place == m, wanted, -1) == own) for m in range(4)], axis=1
    )

    def chunk(s, m):
        if m < PER:
            return q_ref[:, s * QW + m * HEAD : s * QW + (m + 1) * HEAD]
        if m == PER:
            return k_ref[:, s * HEAD : (s + 1) * HEAD]
        at = s * QW + (m - PER - 1) * HEAD
        return (coef * g_ref[:, at : at + HEAD].astype(F32)).astype(BF)

    flat = out_ref.reshape(16, NS, 44, HEAD)
    for begin in (0, 4, 7):
        rhs = jnp.concatenate(
            [
                jnp.concatenate([chunk(s, begin + m) for m in range(4)], axis=0)
                for s in range(NS)
            ],
            axis=1,
        )
        res = mm(onehot, rhs).astype(BF)
        for s in range(NS):
            flat[:, s, 4 * begin : 4 * begin + 16, :] = res[:, s * HEAD : (s + 1) * HEAD].reshape(
                16, 16, HEAD
            )


def pack_rows(slots, coef, q, k, g):
    return pl.pallas_call(
        pack_rows_kernel,
        grid=(4,),
        out_shape=jax.ShapeDtypeStruct((NDP, NS, 11, CAP, HEAD), BF),
        in_specs=[
            pl.BlockSpec((1, ROWS), lambda i: (0, 0)),
            pl.BlockSpec((1, ROWS), lambda i: (0, 0)),
            pl.BlockSpec((ROWS, NS * QW), lambda i: (0, 0)),
            pl.BlockSpec((ROWS, NS * HEAD), lambda i: (0, 0)),
            pl.BlockSpec((ROWS, NS * QW), lambda i: (0, 0)),
        ],
        out_specs=pl.BlockSpec((16, NS, 11, CAP, HEAD), lambda i: (i, 0, 0, 0, 0)),
        compiler_params=params(SMALL),
        cost_estimate=cost(1.6e9, 5e6),
        name="pack_rows",
    )(slots, coef, q, k, g)


def values_kernel(place_ref, slot_ref, x_ref, *refs):
    pieces, (out_ref, w_ref) = refs[: NX * NC], refs[NX * NC :]
    block = w_ref.shape[0] // NDP
    for dx in range(NX):
        for dc in range(NC):
            at = lax.rem(place_ref[0] - dx + NX, NX) * NC + lax.rem(place_ref[1] + dc, NC)
            for held in range(NZ):
                at_z = (held % 2) * 4 + jnp.bitwise_xor(place_ref[2] % 4, held // 2)
                start = pl.multiple_of((at_z * NX * NC + at) * block, 16)
                w_ref[pl.ds(start, block), :] = pieces[dx * NC + dc][held]
    row = lax.broadcasted_iota(jnp.int32, (NDP * 16, 1), 0)
    wanted = (row // 16) * CAP + row % 4
    of_seq = (row % 16) // 4
    value = mm(x_ref[...], w_ref[...]).astype(BF)
    spread = jnp.concatenate(
        [
            ones_where(jnp.where(of_seq == s, wanted, -1) == slot_ref[s : s + 1, :])
            for s in range(NS)
        ],
        axis=1,
    )
    out_ref[...] = mm(spread, value).astype(BF).reshape(NDP, 16, HEAD)


def values_of(place, slots, x_all, pieces):
    depth = x_all.shape[1]
    return pl.pallas_call(
        values_kernel,
        out_shape=(
            jax.ShapeDtypeStruct((NDP, 16, HEAD), BF),
            jax.ShapeDtypeStruct((depth, HEAD), BF),
        ),
        in_specs=[SMEM] + [VMEM] * (2 + NX * NC),
        out_specs=(VMEM, VMEM),
        compiler_params=params(BIG),
        cost_estimate=cost(0.8e9, 8e6),
        name="values",
    )(place, slots, x_all, *pieces)


def turn_kernel(x_ref, out_ref):
    out_ref[...] = x_ref[...].T


def turn(x_all):
    depth = x_all.shape[1]
    width = depth // NZ
    return pl.pallas_call(
        turn_kernel,
        grid=(NZ,),
        out_shape=jax.ShapeDtypeStruct((depth, GROUP), BF),
        in_specs=[pl.BlockSpec((GROUP, width), lambda i: (0, i))],
        out_specs=pl.BlockSpec((width, GROUP), lambda i: (i, 0)),
        compiler_params=params(),
        cost_estimate=cost(1e6, 11e6),
        name="turn",
    )(x_all)


def window(s):
    return max(0, s - 2) * ROWS, (s + 1) * ROWS


def probs_kernel(len_ref, slot_ref, r_ref, v_ref, *refs):
    outs, (both, qs, ks, ds, p0, p1, p2, p3, dv, sems) = refs[:8], refs[8:]
    both_out, qs_out, ks_out, ds_out = outs[:4]
    copies = []

    def send(src, dst):
        copy = pltpu.make_async_copy(src, dst, sems.at[len(copies)])
        copy.start()
        copies.append(copy)

    both[:, 0:16, :] = v_ref[...]
    lane = lax.broadcasted_iota(jnp.int32, (1, NDP * 16), 1)
    wanted = (lane // 16) * CAP + lane % 4
    place = (lane % 16) // 4
    flat = r_ref.reshape(NDP, NS, 44, HEAD)
    for s in range(NS):
        own = slot_column(slot_ref[s : s + 1, :])
        pick = jnp.concatenate(
            [ones_where(jnp.where(place == m, wanted, -1) == own) for m in range(4)], axis=0
        )
        rhs = jnp.concatenate(
            [flat[:, s, 4 * b : 4 * b + 16, :].reshape(NDP * 16, HEAD) for b in (0, 4, 7)],
            axis=1,
        )
        res = mm(pick, rhs).astype(BF)
        qs[s, 0:512, :] = res[:, 0:128]
        qs[s, 512:640, :] = res[0:128, 128:256]
        ks[s * ROWS : (s + 1) * ROWS, :] = res[128:256, 128:256]
        ds[s, 0:256, :] = res[256:512, 128:256]
        ds[s, 256:640, :] = res[128:512, 256:384]
        send(qs.at[s], qs_out.at[s])
        send(ds.at[s], ds_out.at[s])
    send(ks, ks_out)

    first, second = len_ref[0], len_ref[0] + len_ref[1]
    dv[...] = jnp.zeros_like(dv)
    for s, p_ref in enumerate((p0, p1, p2, p3)):
        lo, hi = window(s)
        width = hi - lo
        q_pos = s * ROWS + lax.broadcasted_iota(jnp.int32, (ROWS, width), 0)
        k_pos = lo + lax.broadcasted_iota(jnp.int32, (ROWS, width), 1)
        begin = jnp.where(q_pos >= second, second, jnp.where(q_pos >= first, first, 0))
        visible = (k_pos <= q_pos) & (k_pos >= begin)
        scores = mm_nt(qs[s], ks[lo:hi, :]).reshape(PER, ROWS, width) * SCALE
        scores = jnp.where(visible[None], scores, -jnp.inf)
        weights = jnp.exp(scores - jnp.max(scores, axis=2, keepdims=True))
        probs = weights / jnp.sum(weights, axis=2, keepdims=True)
        half = probs.astype(BF).reshape(PER * ROWS, width)
        p_ref[...] = half
        send(p_ref, outs[4 + s])
        dv[lo:hi, :] += mm_tn(half, ds[s])

    row = lax.broadcasted_iota(jnp.int32, (NDP * 16, 1), 0)
    wanted = (row // 16) * CAP + row % 4
    of_seq = (row % 16) // 4
    spread = jnp.concatenate(
        [
            ones_where(jnp.where(of_seq == s, wanted, -1) == slot_ref[s : s + 1, :])
            for s in range(NS)
        ],
        axis=1,
    )
    both[:, 16:32, :] = mm(spread, dv[...].astype(BF)).astype(BF).reshape(NDP, 16, HEAD)
    send(both, both_out)
    for copy in copies:
        copy.wait()


def probs_of(lengths, slots, r, v):
    shapes = [
        (NDP, 32, HEAD),
        (NS, PER * ROWS, HEAD),
        (GROUP, HEAD),
        (NS, PER * ROWS, HEAD),
    ] + [(PER * ROWS, window(s)[1] - window(s)[0]) for s in range(NS)]
    return pl.pallas_call(
        probs_kernel,
        out_shape=tuple(jax.ShapeDtypeStruct(shape, BF) for shape in shapes),
        in_specs=[SMEM, VMEM, VMEM, VMEM],
        out_specs=(HBM,) * len(shapes),
        scratch_shapes=[pltpu.VMEM(shape, BF) for shape in shapes]
        + [pltpu.VMEM((GROUP, HEAD), F32), pltpu.SemaphoreType.DMA((3 * NS + 2,))],
        compiler_params=params(BIG),
        cost_estimate=cost(3e9, 9e6),
        name="probs",
    )(lengths, slots, r, v)


def grads_kernel(slot_ref, r_ref, *refs):
    kept, dqk_out, held = refs[:7], refs[7], refs[8:15]
    qs, ks, ds = held[:3]
    out, vs, dq, dk, in_sems, out_sems = refs[15:]
    arrivals = [
        pltpu.make_async_copy(kept[n], held[n], in_sems.at[n]) for n in (2, 1, 0, 3, 4, 5, 6)
    ]
    for copy in arrivals:
        copy.start()
    lane = lax.broadcasted_iota(jnp.int32, (1, NDP * 16), 1)
    wanted = (lane // 16) * CAP + lane % 4
    of_seq = (lane % 16) // 4
    pick = jnp.concatenate(
        [
            ones_where(jnp.where(of_seq == s, wanted, -1) == slot_column(slot_ref[s : s + 1, :]))
            for s in range(NS)
        ],
        axis=0,
    )
    vs[...] = mm(pick, r_ref[:, 0:16, :].reshape(NDP * 16, HEAD)).astype(BF)
    dk[...] = jnp.zeros_like(dk)
    for copy in arrivals:
        copy.wait()
    for s in range(NS):
        lo, hi = window(s)
        probs = held[3 + s][...].astype(F32)
        dprobs = mm_nt(ds[s], vs[lo:hi, :])
        delta = jnp.sum(probs * dprobs, axis=1, keepdims=True)
        dscores = (probs * (dprobs - delta)).astype(BF)
        dq[s] = (mm(dscores, ks[lo:hi, :]) * SCALE).astype(BF)
        dk[lo:hi, :] += mm_tn(dscores, qs[s])

    row = lax.broadcasted_iota(jnp.int32, (NDP * 8, 1), 0)
    wanted = (row // 8) * CAP + row % 4
    place = (row % 8) // 4
    for s in range(NS):
        own = slot_ref[s : s + 1, :]
        spread = jnp.concatenate(
            [ones_where(jnp.where(place == m, wanted, -1) == own) for m in range(2)], axis=1
        )
        own_k = (dk[s * ROWS : (s + 1) * ROWS, :] * SCALE).astype(BF)
        rhs = jnp.concatenate(
            [
                dq[s, 0:256, :],
                dq[s, 256:512, :],
                jnp.concatenate([dq[s, 512:640, :], own_k], axis=0),
            ],
            axis=1,
        )
        res = mm(spread, rhs)
        for t in range(3):
            out[s, :, 8 * t : 8 * t + 8, :] = (
                res[:, t * HEAD : (t + 1) * HEAD].reshape(NDP, 8, HEAD).astype(BF)
            )
        pltpu.make_async_copy(out.at[s], dqk_out.at[:, s], out_sems.at[s]).start()
    for s in range(NS):
        pltpu.make_async_copy(out.at[s], dqk_out.at[:, s], out_sems.at[s]).wait()


def grads_of(slots, r, kept):
    return pl.pallas_call(
        grads_kernel,
        out_shape=jax.ShapeDtypeStruct((NDP, NS, 24, HEAD), BF),
        in_specs=[VMEM] * 2 + [HBM] * len(kept),
        out_specs=HBM,
        scratch_shapes=[pltpu.VMEM(one.shape, BF) for one in kept]
        + [
            pltpu.VMEM((NS, NDP, 24, HEAD), BF),
            pltpu.VMEM((GROUP, HEAD), BF),
            pltpu.VMEM((NS, PER * ROWS, HEAD), BF),
            pltpu.VMEM((GROUP, HEAD), F32),
            pltpu.SemaphoreType.DMA((len(kept),)),
            pltpu.SemaphoreType.DMA((NS,)),
        ],
        compiler_params=params(SMALL),
        cost_estimate=cost(3e9, 8e6),
        name="grads",
    )(slots, r, *kept)


def weight_terms_kernel(slot_ref, r_ref, x_ref, dv_ref, out_ref):
    @pl.when(pl.program_id(0) == 0)
    def _():
        lane = lax.broadcasted_iota(jnp.int32, (1, NDP * 16), 1)
        wanted = (lane // 16) * CAP + lane % 4
        of_seq = (lane % 16) // 4
        pick = []
        for s in range(NS):
            own = slot_column(slot_ref[s : s + 1, :])
            pick.append(ones_where(jnp.where(of_seq == s, wanted, -1) == own))
        rows = r_ref[...].reshape(NDP * 16, HEAD)
        dv_ref[...] = mm(jnp.concatenate(pick, axis=0), rows).astype(BF)

    terms = mm(x_ref[...], dv_ref[...]).astype(BF)
    block = out_ref.shape[3]
    for z in range(out_ref.shape[2]):
        for x in range(NX):
            for c in range(NC):
                at = ((z * NX + x) * NC + c) * block
                out_ref[c, x, z] = terms[at : at + block, :]


def weight_terms(slots, r, x_turned):
    block = x_turned.shape[0] // NDP
    steps = 4
    each = NZ // steps
    return pl.pallas_call(
        weight_terms_kernel,
        grid=(steps,),
        out_shape=(
            jax.ShapeDtypeStruct((GROUP, HEAD), BF),
            jax.ShapeDtypeStruct((NC, NX, NZ, block, HEAD), BF),
        ),
        in_specs=[
            pl.BlockSpec((NS, ROWS), lambda i: (0, 0)),
            pl.BlockSpec((NDP, 16, HEAD), lambda i: (0, 1, 0)),
            pl.BlockSpec((each * NX * NC * block, GROUP), lambda i: (i, 0)),
        ],
        out_specs=(
            pl.BlockSpec((GROUP, HEAD), lambda i: (0, 0)),
            pl.BlockSpec((NC, NX, each, block, HEAD), lambda i: (0, 0, i, 0, 0)),
        ),
        compiler_params=params(),
        cost_estimate=cost(0.8e9, 7e6),
        name="weight_terms",
    )(slots, r, x_turned)


def grad_x_kernel(dv_ref, w_ref, out_ref):
    dv = jnp.concatenate([dv_ref[s] for s in range(NS)], axis=1)
    w = jnp.concatenate([w_ref[s] for s in range(NS)], axis=1)
    out_ref[...] = mm_nt(dv, w).astype(BF)


def grad_x_of(dv, w):
    depth = w.shape[1]
    width = 1024
    return pl.pallas_call(
        grad_x_kernel,
        grid=(depth // width,),
        out_shape=jax.ShapeDtypeStruct((ROWS, depth), BF),
        in_specs=[
            pl.BlockSpec((NS, ROWS, HEAD), lambda i: (0, 0, 0)),
            pl.BlockSpec((NS, width, HEAD), lambda i: (0, i, 0)),
        ],
        out_specs=pl.BlockSpec((ROWS, width), lambda i: (0, i)),
        compiler_params=params(),
        cost_estimate=cost(0.7e9, 7e6),
        name="grad_x",
    )(dv, w)


def unpack_kernel(slot_ref, r_ref, q_ref, k_ref):
    lane = lax.broadcasted_iota(jnp.int32, (1, NDP * 8), 1)
    wanted = (lane // 8) * CAP + lane % 4
    place = (lane % 8) // 4
    own = slot_column(slot_ref[...])
    pick = jnp.concatenate(
        [ones_where(jnp.where(place == m, wanted, -1) == own) for m in range(2)], axis=0
    )
    for s in range(NS):
        rhs = jnp.concatenate(
            [
                r_ref[:, s, 8 * t : 8 * t + 8, :].astype(F32).reshape(NDP * 8, HEAD).astype(BF)
                for t in range(3)
            ],
            axis=1,
        )
        res = mm(pick, rhs).astype(BF)
        for m in range(PER):
            t, at = m // 2, (m % 2) * ROWS
            q_ref[:, s * QW + m * HEAD : s * QW + (m + 1) * HEAD] = res[
                at : at + ROWS, t * HEAD : (t + 1) * HEAD
            ]
        k_ref[:, s * HEAD : (s + 1) * HEAD] = res[ROWS : 2 * ROWS, 2 * HEAD : 3 * HEAD]


def unpack(slots, r):
    return pl.pallas_call(
        unpack_kernel,
        out_shape=(
            jax.ShapeDtypeStruct((ROWS, NS * QW), BF),
            jax.ShapeDtypeStruct((ROWS, NS * HEAD), BF),
        ),
        in_specs=[VMEM, VMEM],
        out_specs=(VMEM, VMEM),
        compiler_params=params(),
        cost_estimate=cost(0.5e9, 4e6),
        name="unpack",
    )(slots, r)


def dp_of(z, x, c):
    return (z * NX + x) * NC + c


EACH = [(z, x, c) for z in range(NZ) for x in range(NX) for c in range(NC)]


def along_z(value, d):
    return lax.ppermute(value, "dp", [(dp_of(z, x, c), dp_of((z + d) % NZ, x, c)) for z, x, c in EACH])


def along_x(value, d):
    return lax.ppermute(value, "dp", [(dp_of(z, x, c), dp_of(z, (x + d) % NX, c)) for z, x, c in EACH])


def along_c(value):
    return lax.ppermute(value, "dp", [(dp_of(z, x, c), dp_of(z, x, 1 - c)) for z, x, c in EACH])


def along_seq(value, d):
    return lax.ppermute(value, "seq", [(s, (s + d) % NS) for s in range(NS)])


def rank_of(label, key):
    same = (label[:, None] == label[None, :]) & (key[None, :] < key[:, None])
    return jnp.sum(same.astype(jnp.int32), axis=1)


def in_order(parts, own):
    count = len(parts)
    index = jnp.arange(count, dtype=jnp.int32).reshape((count,) + (1,) * parts[0].ndim)
    total = jnp.zeros((count,) + parts[0].shape, parts[0].dtype)
    for d, part in enumerate(parts):
        total = jnp.where(index == (own - d) % count, part[None], total)
    return total


def shards(
    x_saved, q_saved, k_saved, grad_attn, token_coef, dest_of, source_of, lengths, value_weight
):
    dp, seq = lax.axis_index("dp"), lax.axis_index("seq")
    z, x, c = dp // (NX * NC), (dp // NC) % NX, dp % NC

    def pick(value, at):
        return lax.dynamic_index_in_dim(value, at, 0, keepdims=False)

    target = dest_of // GROUP
    send_slot = target * CAP + rank_of(target, jnp.arange(ROWS, dtype=jnp.int32))
    anchor = source_of // GROUP
    recv_slot = anchor * CAP + rank_of(anchor, source_of)
    slots = jnp.stack([send_slot, recv_slot])

    def across_z(value, bits):
        swap = [(dp_of(a, b, e), dp_of(a ^ bits, b, e)) for a, b, e in EACH]
        return lax.ppermute(value, "dp", swap)

    own_w = lax.dynamic_slice_in_dim(value_weight, seq * HEAD, HEAD, axis=1)
    far_w = across_z(own_w, 4)
    low = z < 4
    stage = jnp.stack([jnp.where(low, own_w, far_w), jnp.where(low, far_w, own_w)])
    stage = jnp.concatenate([stage] + [across_z(stage, bits) for bits in (1, 2, 3)], axis=0)

    own_slot = send_slot[None]
    rows = pack_rows(own_slot, token_coef[None], q_saved, k_saved, grad_attn)
    rows, slots, stage = lax.optimization_barrier((rows, slots, stage))
    arrived = lax.all_to_all(
        rows.reshape(NDP * NS, 11, CAP, HEAD), ("dp", "seq"), split_axis=0, concat_axis=0, tiled=True
    )

    all_slots = in_order([slots] + [along_seq(slots, d) for d in range(1, NS)], seq)
    send_all, recv_all = all_slots[:, 0], all_slots[:, 1]
    x_all = lax.all_gather(x_saved, "seq", axis=0, tiled=True)

    pieces = []
    for part in [stage] + [along_x(stage, d) for d in range(1, NX)]:
        pieces += [part, along_c(part)]
    place = jnp.stack([x, c, z]).astype(jnp.int32)
    v_out, head_w = values_of(place, send_all, x_all, pieces)
    w_all = lax.all_gather(head_w, "seq", axis=0, tiled=True)

    arrived, recv_all, v_out = lax.optimization_barrier((arrived, recv_all, v_out))
    both, *kept = probs_of(lengths[0], recv_all, arrived.reshape(NDP, NS, 11, CAP, HEAD), v_out)
    both = lax.all_to_all(both, "dp", split_axis=0, concat_axis=0, tiled=True)
    x_turned = turn(x_all)
    both, x_turned = lax.optimization_barrier((both, x_turned))
    dqk_out = grads_of(recv_all, both, kept)
    dqk_out, send_all = lax.optimization_barrier((dqk_out, send_all))
    dv_head, terms = weight_terms(send_all, both, x_turned)

    dqk_back = lax.all_to_all(
        dqk_out.reshape(NDP * NS, 24, HEAD), ("dp", "seq"), split_axis=0, concat_axis=0, tiled=True
    )

    part = pick(terms, c).astype(F32) + along_c(pick(terms, 1 - c)).astype(F32)
    part = part.astype(BF)
    total = pick(part, x).astype(F32)
    for d in range(1, NX):
        total = total + along_x(pick(part, (x + d) % NX), d).astype(F32)
    dv_view = dv_head.reshape(NS, ROWS, HEAD)
    dv_parts = [pick(dv_view, seq)]
    for d in range(1, NS):
        dv_parts.append(along_seq(pick(dv_view, (seq + d) % NS), d))
    grad_x = grad_x_of(in_order(dv_parts, seq), w_all.reshape(NS, -1, HEAD))

    half = total.astype(BF).reshape(NZ // 2, 2, *total.shape[1:])
    keep = lax.dynamic_index_in_dim(half, z % 2, 1, keepdims=False)
    give = lax.dynamic_index_in_dim(half, 1 - z % 2, 1, keepdims=False)
    half = (keep.astype(F32) + across_z(give, 1).astype(F32)).astype(BF)
    half, grad_x, dqk_back = lax.optimization_barrier((half, grad_x, dqk_back))
    total = pick(half, z // 2).astype(F32)
    for bits in (1, 2, 3):
        total = total + across_z(pick(half, (z // 2) ^ bits), 2 * bits).astype(F32)
    own = total / math.sqrt(GROUP * NDP)
    grad_q, grad_k = unpack(own_slot, dqk_back.reshape(NDP, NS, 24, HEAD))
    own, grad_q, grad_k = lax.optimization_barrier((own, grad_q, grad_k))
    heads = in_order([own] + [along_seq(own, d) for d in range(1, NS)], seq)
    grad_v_weight = jnp.concatenate([heads[s] for s in range(NS)], axis=1)

    return (grad_x, grad_q, grad_k, grad_v_weight)


def solution(mesh):
    rows = P(("dp", "seq"), None)
    flat = P(("dp", "seq"))
    whole = P("dp", None)
    return jax.shard_map(
        shards,
        mesh=mesh,
        in_specs=(rows, rows, rows, rows, flat, flat, flat, whole, whole),
        out_specs=(rows, rows, rows, whole),
        check_vma=False,
    )
```
